256 devices in a mesh: ctx: 64 (over y, z_hi, x), head: 4 (over z_lo, core).
Axes of the slice: x: 4, y: 4, z: 8 (z_hi: 4, z_lo: 2; z = z_hi * 2 + z_lo), core: 2. Of those that a mesh axis runs over, the one named last changes fastest.
Arguments:
- long_qkv: bfloat16 [3, 8192, 5120], P(None, 'ctx', 'head'), may hold values from -640 to 640
- long_grad: bfloat16 [8192, 5120], P('ctx', 'head'), may hold values from -24 to 24
- short_qkv: bfloat16 [3, 8192, 5120], P(None, 'ctx', 'head'), may hold values from -640 to 640
- short_grad: bfloat16 [8192, 5120], P('ctx', 'head'), may hold values from -24 to 24
- short_lengths: int32 [256], replicated, may hold values from 1 to 64, 8192 in all
- norm_gains: float32 [2, 5120], P(None, 'head'), may hold values from 0.25 to 1.75
Outputs:
- long_out: bfloat16 [8192, 5120], P('ctx', 'head')
- long_dqkv: bfloat16 [3, 8192, 5120], P(None, 'ctx', 'head')
- short_out: bfloat16 [8192, 5120], P('ctx', 'head')
- short_dqkv: bfloat16 [3, 8192, 5120], P(None, 'ctx', 'head')
The draws below stay inside these ranges and needn't reach their ends.
Inputs may be any that keep to these rules, and one draw needn't show every extreme that they name: `short_lengths`: the 256 short documents lie end to end in this order over the 8192 short tokens.
All inputs are finite; a program needn't handle non-finite values.
Results may differ from the reference program's by a relative error of at most 0.012.
The reference program's roundings to bfloat16 on the way (of `weights` and `score_grad`) count: a program that leaves them out, or rounds other values in their place, can miss the bound.
Values may be sent and summed in bfloat16 or wider, within the bound.
A program may use at most 128 MiB of HBM per device.

```python
import math
import jax
import jax.numpy as jnp
import numpy as np
from jax import lax

HEADS = 40
HEAD_DIM = 128
SPAN = 8
LONG_DEV = 128
SHORT_DEV = 128
WIDTH = 5120
DOC_MAX = 64
LONG = 8192
SHORT = 8192
NDOCS = 256
N_CTX = 64


def fill_projections(base_key, salt, row_count, column_ramp, uniform_share):
    full_width = HEADS * HEAD_DIM
    subkeys = jax.random.split(jax.random.fold_in(base_key, salt), 7)
    full_shape = (3, row_count, full_width)
    normal_part = jnp.clip(jax.random.normal(subkeys[0], full_shape, jnp.float32), -4.0, 4.0)
    raw_noise = normal_part
    column = jnp.arange(full_width, dtype=jnp.float32) / (full_width - 1)
    column_scale = column_ramp ** column * jnp.exp(jax.random.uniform(subkeys[2], (full_width,), jnp.float32, 0.0, jnp.log(4.0)))
    row_scale = jnp.exp(jax.random.uniform(subkeys[3], (2, row_count, 1), jnp.float32, 0.0, jnp.log(10.0)))
    unit_scale = column_scale / (2.0 * column_ramp ** 0.5)
    query_dir = raw_noise[0] * unit_scale
    key_dir = raw_noise[1] * unit_scale
    scaled = raw_noise[:2] * column_scale * row_scale
    row_index = jnp.arange(row_count)
    block_id = row_index // 64
    in_block = row_index % 64
    chosen = block_id % HEADS
    inside = (jnp.arange(full_width) // HEAD_DIM)[None, :] == chosen[:, None]
    pattern = jnp.clip(jax.random.normal(subkeys[4], (row_count // 64, HEAD_DIM), jnp.float32), -4.0, 4.0)
    repeated = jnp.tile(pattern, (1, HEADS))[block_id]
    leakage = jnp.exp(jax.random.uniform(subkeys[5], (row_count // 64,), jnp.float32, jnp.log(0.13), jnp.log(0.3)))[block_id]
    nudge_rows = jnp.where((in_block == 2)[:, None], 0.09 * normal_part[2], 0.0)
    aligned = jnp.where(inside, repeated + nudge_rows, leakage[:, None] * normal_part[0])
    query_pick = (in_block == 63)[:, None] & (uniform_share > 0.5)
    key_pick = ((in_block == 1) | (in_block == 2))[:, None] & (uniform_share > 0.5)
    queries = jnp.where(query_pick, aligned, scaled[0])
    key_rows = jnp.where(key_pick, aligned, scaled[1])
    value_rows = 0.5 * key_dir + 0.85 * raw_noise[2]
    grad_normal = jnp.clip(jax.random.normal(subkeys[6], (row_count, full_width), jnp.float32), -4.0, 4.0)
    cotangent = 0.6 * query_dir + 0.8 * grad_normal
    return (jnp.stack([queries, key_rows, value_rows]).astype(jnp.bfloat16), cotangent.astype(jnp.bfloat16))


def draw_long_qkv(key, part):
    return fill_projections(key, 5, LONG, 3.0, 0.0)[0]


def draw_long_grad(key, part):
    return fill_projections(key, 5, LONG, 3.0, 0.0)[1]


def draw_short_qkv(key, part):
    return fill_projections(key, 9, SHORT, 3.0, 0.0)[0]


def draw_short_grad(key, part):
    return fill_projections(key, 9, SHORT, 3.0, 0.0)[1]


def length_profile(amount, total, most, lean):
    weights = [(1 << 20) // math.isqrt(grade ** lean) + 1 for grade in range(2, amount + 1)]
    spare, holding = total - most - (amount - 1), [1] * (amount - 1)
    while spare > 0:
        free = [i for i in range(amount - 1) if holding[i] < most]
        pool, remaining = sum([weights[i] for i in free]), spare
        for i in free:
            more = min(most - holding[i], max(1, remaining * weights[i] // pool), spare)
            holding[i] = holding[i] + more
            spare = spare - more
    return np.array([most] + holding)


def ragged(own_key, number_of, total, reach, slope):
    if number_of == 2:
        one = jax.random.randint(own_key, (), max(1, total - reach), min(reach, total - 1) + 1)
        return jnp.stack([one, total - one])
    tallies = jnp.asarray(length_profile(number_of, total, reach, slope), jnp.int32)
    pairs = (number_of - 1) // 2
    donor, taker = tallies[1:1 + 2 * pairs:2], tallies[2:2 + 2 * pairs:2]
    room = jnp.minimum(donor - 1, reach - taker)
    moved = jax.random.randint(jax.random.fold_in(own_key, 1), (pairs,), 0, 1 << 20) % (room + 1)
    tallies = tallies.at[1:1 + 2 * pairs:2].set(donor - moved).at[2:2 + 2 * pairs:2].set(taker + moved)
    return tallies[jax.random.permutation(jax.random.fold_in(own_key, 2), number_of)]


def setup_inputs(seed: int = 0) -> dict:
    keys = jax.random.split(jax.random.key(seed), 7)
    return {
        "long_qkv": draw_long_qkv(jax.random.fold_in(keys[6], 71), 0),
        "long_grad": draw_long_grad(jax.random.fold_in(keys[6], 71), 0),
        "short_qkv": draw_short_qkv(jax.random.fold_in(keys[6], 71), 0),
        "short_grad": draw_short_grad(jax.random.fold_in(keys[6], 71), 0),
        "short_lengths": ragged(keys[4], NDOCS, SHORT, DOC_MAX, 2).astype(jnp.int32),
        "norm_gains": jnp.clip(1.0 + 0.15 * jax.random.normal(keys[5], (2, WIDTH), jnp.float32), 0.25, 1.75),
    }


EPSILON = 1e-06
NEGATIVE = -1e+30

def norm_rows(matrix, gain_row):
    widened = matrix.astype(jnp.float32)
    inverse = lax.rsqrt(lax.optimization_barrier(jnp.sum(widened * widened, axis=1, keepdims=True)) / WIDTH + EPSILON)
    return ((widened * inverse * gain_row).astype(jnp.bfloat16), inverse)

def norm_back(matrix, gain_row, inverse, gradient):
    widened = matrix.astype(jnp.float32)
    inner_sum = lax.optimization_barrier(jnp.sum(gradient * gain_row * widened, axis=1, keepdims=True))
    return (inverse * gain_row * gradient - widened * (inverse * inverse * inverse) * inner_sum / WIDTH).astype(jnp.bfloat16)

def attend_head(queries, key_rows, value_rows, cotangent, allowed):
    factor = HEAD_DIM ** (-0.5)
    scores = jnp.where(allowed, jnp.dot(queries, key_rows.T, preferred_element_type=jnp.float32) * factor, NEGATIVE)
    highest = lax.optimization_barrier(jnp.max(scores, axis=1, keepdims=True))
    log_total = highest + jnp.log(lax.optimization_barrier(jnp.sum(jnp.exp(scores - highest), axis=1, keepdims=True)))
    probability = jnp.exp(scores - log_total)
    weights = probability.astype(jnp.bfloat16)
    output = jnp.dot(weights, value_rows, preferred_element_type=jnp.float32).astype(jnp.bfloat16)
    row_dot = lax.optimization_barrier(jnp.sum(cotangent.astype(jnp.float32) * output.astype(jnp.float32), axis=1, keepdims=True))
    weight_grad = jnp.dot(cotangent, value_rows.T, preferred_element_type=jnp.float32)
    score_grad = (probability * (weight_grad - row_dot)).astype(jnp.bfloat16)
    query_grad = jnp.dot(score_grad, key_rows, preferred_element_type=jnp.float32) * factor
    key_grad = jnp.dot(score_grad.T, queries, preferred_element_type=jnp.float32) * factor
    value_grad = jnp.dot(weights.T, cotangent, preferred_element_type=jnp.float32)
    return (output, query_grad, key_grad, value_grad)

def head_major(matrix):
    return jnp.transpose(matrix.reshape(matrix.shape[0], HEADS, HEAD_DIM), (1, 0, 2))

def row_major(stacked):
    return jnp.transpose(stacked, (1, 0, 2)).reshape(stacked.shape[1], WIDTH)

def attend(queries, key_rows, value_rows, cotangent, allowed):

    def one_head(group):
        return attend_head(group[0], group[1], group[2], group[3], allowed)
    results = lax.map(one_head, (head_major(queries), head_major(key_rows), head_major(value_rows), head_major(cotangent)))
    return tuple((row_major(piece) for piece in results))

def segment_of(positions, doc_ends):
    counted = lax.optimization_barrier(jnp.sum((positions[:, None] >= doc_ends[None, :]).astype(jnp.int32), axis=1, dtype=jnp.int32))
    return jnp.where(positions >= 0, counted, -1)

def reference(long_qkv, long_grad, short_qkv, short_grad, short_lengths, norm_gains):
    long_q, long_q_inv = norm_rows(long_qkv[0], norm_gains[0])
    long_k, long_k_inv = norm_rows(long_qkv[1], norm_gains[1])
    doc_rows = SPAN * LONG_DEV
    doc_count = LONG // doc_rows
    causal = jnp.arange(doc_rows)[:, None] >= jnp.arange(doc_rows)[None, :]

    def one_doc(group):
        return attend(group[0], group[1], group[2], group[3], causal)

    def shaped(matrix):
        return matrix.reshape(doc_count, doc_rows, WIDTH)
    long_output, long_dq, long_dk, long_dv = lax.map(one_doc, (shaped(long_q), shaped(long_k), shaped(long_qkv[2]), shaped(long_grad)))
    long_out = long_output.reshape(LONG, WIDTH)
    long_dqkv = jnp.stack([norm_back(long_qkv[0], norm_gains[0], long_q_inv, long_dq.reshape(LONG, WIDTH)), norm_back(long_qkv[1], norm_gains[1], long_k_inv, long_dk.reshape(LONG, WIDTH)), long_dv.reshape(LONG, WIDTH).astype(jnp.bfloat16)])
    short_q, short_q_inv = norm_rows(short_qkv[0], norm_gains[0])
    short_k, short_k_inv = norm_rows(short_qkv[1], norm_gains[1])
    doc_ends = jnp.cumsum(short_lengths, dtype=jnp.int32)
    padded_k = jnp.concatenate([jnp.zeros((DOC_MAX, WIDTH), jnp.bfloat16), short_k], axis=0)
    padded_v = jnp.concatenate([jnp.zeros((DOC_MAX, WIDTH), jnp.bfloat16), short_qkv[2]], axis=0)
    positions = jnp.arange(SHORT + DOC_MAX, dtype=jnp.int32) - DOC_MAX
    padded_seg = segment_of(positions, doc_ends)
    window = SHORT_DEV + DOC_MAX

    def one_block(block_index):
        first_row = (block_index * SHORT_DEV).astype(jnp.int32)
        queries = lax.dynamic_slice_in_dim(short_q, first_row, SHORT_DEV, 0)
        cotangent = lax.dynamic_slice_in_dim(short_grad, first_row, SHORT_DEV, 0)
        key_rows = lax.dynamic_slice_in_dim(padded_k, first_row, window, 0)
        value_rows = lax.dynamic_slice_in_dim(padded_v, first_row, window, 0)
        query_seg = lax.dynamic_slice_in_dim(padded_seg, first_row + DOC_MAX, SHORT_DEV, 0)
        key_seg = lax.dynamic_slice_in_dim(padded_seg, first_row, window, 0)
        query_pos = first_row + jnp.arange(SHORT_DEV, dtype=jnp.int32)
        key_pos = first_row - DOC_MAX + jnp.arange(window, dtype=jnp.int32)
        allowed = (query_seg[:, None] == key_seg[None, :]) & (key_pos[None, :] <= query_pos[:, None])
        return attend(queries, key_rows, value_rows, cotangent, allowed)
    short_output, short_dq, short_dk, short_dv = lax.map(one_block, jnp.arange(N_CTX, dtype=jnp.int32))

    def fold_rim(parts):
        own_rows = parts[:, DOC_MAX:]
        arrived = jnp.concatenate([parts[1:, :DOC_MAX], jnp.zeros((1, DOC_MAX, WIDTH), parts.dtype)], axis=0)
        joined = jnp.concatenate([own_rows[:, :SHORT_DEV - DOC_MAX], own_rows[:, SHORT_DEV - DOC_MAX:] + arrived], axis=1)
        return joined.reshape(SHORT, WIDTH)
    short_out = short_output.reshape(SHORT, WIDTH)
    short_dqkv = jnp.stack([norm_back(short_qkv[0], norm_gains[0], short_q_inv, short_dq.reshape(SHORT, WIDTH)), norm_back(short_qkv[1], norm_gains[1], short_k_inv, fold_rim(short_dk)), fold_rim(short_dv).astype(jnp.bfloat16)])
    return (long_out, long_dqkv, short_out, short_dqkv)
```

```python
import jax
import jax.numpy as jnp
from jax import lax
from jax.experimental import pallas as pl
from jax.experimental.pallas import tpu as pltpu
from jax.sharding import PartitionSpec as P

MESH = pl.DeviceIdType.MESH
BF16 = jnp.bfloat16
F32 = jnp.float32
HEAD_DIM = 128
WIDTH = 5120
DOC_MAX = 64
ROWS = 128
LOCAL = 1280
HEADS = 10
HALF = 512
EPSILON = 1e-06
NEGATIVE = -1e30
FACTOR = HEAD_DIM ** (-0.5)


def first_head(x, core):
    return lax.div(5 * x + 1 - core, 2)


def has_third(x, core):
    return lax.rem(x + core, 2) == 0


def columns(head):
    return pl.ds(pl.multiple_of(head * HEAD_DIM, HEAD_DIM), HEAD_DIM)


def block_rows(x):
    return pl.ds(pl.multiple_of(x * ROWS, ROWS), ROWS)


def await_bytes(ref, sem):
    pltpu.make_async_copy(ref, ref, sem).wait()


def dot(a, b):
    return jnp.dot(a, b, preferred_element_type=F32)


def dot_t(a, b):
    return lax.dot_general(a, b, (((1,), (1,)), ((), ())), preferred_element_type=F32)


def attend(q, do, pieces):
    scores = []
    for k, v, mask in pieces:
        s = dot_t(k, q) * FACTOR
        scores.append(s if mask is None else jnp.where(mask, s, NEGATIVE))
    high = jnp.max(scores[0], axis=0, keepdims=True)
    for s in scores[1:]:
        high = jnp.maximum(high, jnp.max(s, axis=0, keepdims=True))
    powers = [jnp.exp(s - high) for s in scores]
    total = jnp.sum(powers[0], axis=0, keepdims=True)
    for p in powers[1:]:
        total = total + jnp.sum(p, axis=0, keepdims=True)
    log_total = high + jnp.log(total)
    share = 1.0 / total
    probs = [p * share for p in powers]
    weights = [p.astype(BF16) for p in probs]
    out_t = dot(pieces[0][1].T, weights[0])
    for (k, v, mask), w in zip(pieces[1:], weights[1:]):
        out_t = out_t + dot(v.T, w)
    out = out_t.T.astype(BF16)
    row_dot = jnp.sum(do.astype(F32).T * out_t.astype(BF16).astype(F32), axis=0, keepdims=True)
    grads = [
        (p * (dot_t(v, do) - row_dot)).astype(BF16) for (k, v, mask), p in zip(pieces, probs)
    ]
    dq_t = dot(pieces[0][0].T, grads[0])
    for (k, v, mask), g in zip(pieces[1:], grads[1:]):
        dq_t = dq_t + dot(k.T, g)
    return out, (dq_t * FACTOR).T, log_total, row_dot, weights, grads


def to_rows(cols):
    lane = lax.broadcasted_iota(jnp.int32, (ROWS, HEAD_DIM), 1)
    packed = jnp.zeros((ROWS, HEAD_DIM), F32)
    for i, col in enumerate(cols):
        packed = jnp.where(lane == i, col, packed)
    return packed.T[:8]


def to_cols(rows):
    return jnp.concatenate([rows] * (ROWS // 8), axis=0).T


def kernel(
    lqkv, lgrad, sqkv, sgrad, lengths, gains,
    lout, ldqkv, sout, sdqkv,
    raw, nlong, sq, kx, vx, sdo, inv, sums, sums_in,
    t, z, stats, stats_in, g, acc, r, so, sd, rim_out, rim_in, fin,
    load, v_s, v_r, q_s, q_r, z_s, z_r, l_s, l_r, b_s, b_r, h_s, h_r, m_s, m_r, o_s,
):
    c = lax.axis_index("ctx")
    h = lax.axis_index("head")
    x = lax.rem(c, 4)
    row_base = c - x
    par = lax.rem(lax.div(c, 4), 2)
    core = lax.rem(h, 2)
    third = has_third(x, core)
    count = jnp.where(third, 3, 2)
    first = first_head(x, core)
    mate = (c + 4 - 8 * par, h)
    after = (lax.rem(c + 1, 64), h)
    before = (lax.rem(c + 63, 64), h)

    def x_at(d):
        return lax.rem(x + d, 4)

    def x_dev(d):
        return (row_base + x_at(d), h)

    def head_dev(d):
        return (c, lax.rem(h + d, 4))

    def remote(src, dst, send, recv, dev):
        return pltpu.make_async_remote_copy(
            src_ref=src, dst_ref=dst, send_sem=send, recv_sem=recv,
            device_id=dev, device_id_type=MESH,
        )

    loads = [
        pltpu.make_async_copy(lqkv.at[0], raw.at[0], load.at[0]),
        pltpu.make_async_copy(lqkv.at[1], raw.at[1], load.at[1]),
        pltpu.make_async_copy(sqkv.at[0], raw.at[2], load.at[2]),
        pltpu.make_async_copy(sqkv.at[1], raw.at[3], load.at[3]),
        pltpu.make_async_copy(sqkv.at[2], vx.at[pl.ds(DOC_MAX, ROWS)], load.at[4]),
        pltpu.make_async_copy(sgrad, sdo, load.at[5]),
    ]
    for copy in loads:
        copy.start()

    peers = [x_dev(1), x_dev(2), x_dev(3), mate, head_dev(1), head_dev(2), head_dev(3), after, before]
    barrier = pltpu.get_barrier_semaphore()
    for dev in peers:
        pl.semaphore_signal(barrier, inc=1, device_id=dev, device_id_type=MESH)

    mine = block_rows(x)

    def own_values(s):
        for kind, src in ((0, lqkv.at[2]), (1, lgrad)):
            pltpu.make_async_copy(
                src.at[:, columns(first + s)], t.at[s, 2 + kind, mine], v_r.at[kind, s, 0]
            ).start()

    def send_values(s, d):
        for kind, src in ((0, lqkv.at[2]), (1, lgrad)):
            remote(
                src.at[:, columns(first_head(x_at(d), core) + s)], t.at[s, 2 + kind, mine],
                v_s.at[kind, s, d], v_r.at[kind, s, d], x_dev(d),
            ).start()

    def send_keys(s, d):
        remote(
            nlong.at[:, :, columns(first_head(x_at(d), core) + s)], t.at[s, pl.ds(0, 2), mine],
            q_s.at[s, d], q_r.at[s, d], x_dev(d),
        ).start()

    def own_keys(s):
        pltpu.make_async_copy(
            nlong.at[:, :, columns(first + s)], t.at[s, pl.ds(0, 2), mine], q_r.at[s, 0]
        ).start()

    def to_peers(s, send):
        for d in (1, 2, 3):
            if s < 2:
                send(s, d)
            else:
                pl.when(has_third(x_at(d), core))(lambda d=d: send(s, d))

    own_values(0)
    own_values(1)
    pl.when(third)(lambda: own_values(2))

    pl.semaphore_wait(barrier, len(peers))

    to_peers(0, send_values)
    rim_v = remote(
        sqkv.at[2, pl.ds(ROWS - DOC_MAX, DOC_MAX)], vx.at[pl.ds(0, DOC_MAX)],
        m_s.at[0], m_r.at[0], after,
    )
    rim_v.start()

    for copy in loads[:4]:
        copy.wait()

    def square_step(j, sums_so_far):
        cols = columns(j)
        new = []
        for i in range(4):
            w = raw[i, :, cols].astype(F32)
            new.append(sums_so_far[i] + w * w)
        return tuple(new)

    zero = jnp.zeros((ROWS, HEAD_DIM), F32)
    squares = lax.fori_loop(0, HEADS, square_step, (zero,) * 4)
    sums[0] = to_rows([jnp.sum(a, axis=1, keepdims=True) for a in squares])
    for d in (1, 2, 3):
        remote(sums.at[0], sums_in.at[0, d], h_s.at[0, d], h_r.at[0, d], head_dev(d)).start()
    for d in (1, 2, 3):
        await_bytes(sums_in.at[0, d], h_r.at[0, d])
    all_sums = sums[0] + sums_in[0, 1] + sums_in[0, 2] + sums_in[0, 3]
    inv[...] = to_cols(lax.rsqrt(all_sums / WIDTH + EPSILON))

    def normalize_step(j, _):
        cols = columns(j)
        nlong[0, :, cols] = (raw[0, :, cols].astype(F32) * inv[:, 0:1] * gains[0:1, cols]).astype(BF16)
        nlong[1, :, cols] = (raw[1, :, cols].astype(F32) * inv[:, 1:2] * gains[1:2, cols]).astype(BF16)
        sq[:, cols] = (raw[2, :, cols].astype(F32) * inv[:, 2:3] * gains[0:1, cols]).astype(BF16)
        kx[pl.ds(DOC_MAX, ROWS), cols] = (
            raw[3, :, cols].astype(F32) * inv[:, 3:4] * gains[1:2, cols]
        ).astype(BF16)
        return 0

    lax.fori_loop(0, HEADS, normalize_step, 0)

    own_keys(0)
    own_keys(1)
    pl.when(third)(lambda: own_keys(2))
    to_peers(0, send_keys)
    to_peers(1, send_values)
    to_peers(1, send_keys)
    remote(
        kx.at[pl.ds(ROWS, DOC_MAX)], kx.at[pl.ds(0, DOC_MAX)], m_s.at[1], m_r.at[1], after
    ).start()
    to_peers(2, send_values)
    to_peers(2, send_keys)

    diag = lax.broadcasted_iota(jnp.int32, (256, 256), 0) <= lax.broadcasted_iota(
        jnp.int32, (256, 256), 1
    )

    def send_back(s, pair):
        for d in (1, 2, 3):
            remote(
                g.at[s, pl.ds(2 * pair, 2), block_rows(x_at(d))],
                r.at[pl.ds(2 * pair, 2), :, columns(first + s)],
                b_s.at[pair, s, d], b_r.at[pair, s, d], x_dev(d),
            ).start()
        pltpu.make_async_copy(
            g.at[s, pl.ds(2 * pair, 2), mine], r.at[pl.ds(2 * pair, 2), :, columns(first + s)],
            b_r.at[pair, s, 0],
        ).start()

    def relay(s):
        for d in range(4):
            rows = block_rows(lax.rem(x + 4 - d, 4))
            await_bytes(t.at[s, 2, rows], v_r.at[0, s, d])
            await_bytes(t.at[s, 3, rows], v_r.at[1, s, d])
            remote(t.at[s, 2 + par, rows], z.at[s, 0, rows], z_s.at[0, s, d], z_r.at[0, s, d], mate).start()
        for d in range(4):
            rows = block_rows(lax.rem(x + 4 - d, 4))
            await_bytes(t.at[s, pl.ds(0, 2), rows], q_r.at[s, d])
            remote(t.at[s, 1 - par, rows], z.at[s, 1, rows], z_s.at[1, s, d], z_r.at[1, s, d], mate).start()

    def within(s, i, early, keep):
        rows = pl.ds(i * 256, 256)
        q, do = t[s, 0, rows], t[s, 3, rows]
        pieces = list(early)
        if i:
            pieces.append((t[s, 1, pl.ds(0, 256)], t[s, 2, pl.ds(0, 256)], None))
        pieces.append((t[s, 1, rows], t[s, 2, rows], diag))
        out, dq, log_total, row_dot, weights, grads = attend(q, do, pieces)
        g[s, 0, rows] = out
        g[s, 1, rows] = dq.astype(BF16)
        if keep:
            stats[s, 0:1, rows] = log_total
            stats[s, 1:2, rows] = row_dot
        base = len(early)
        if i:
            acc[s, 0, pl.ds(0, 256)] = acc[s, 0, pl.ds(0, 256)] + dot(grads[base], q)
            acc[s, 1, pl.ds(0, 256)] = acc[s, 1, pl.ds(0, 256)] + dot(weights[base], do)
        acc[s, 0, rows] = dot(grads[-1], q)
        acc[s, 1, rows] = dot(weights[-1], do)

    def first_half(s):
        for i in range(2):
            within(s, i, [], False)
        send_back(s, 0)

    def relay_step(s, _):
        relay(s)
        pl.when(par == 0)(lambda: first_half(s))
        return 0

    lax.fori_loop(0, count, relay_step, 0)

    for copy in loads[4:]:
        copy.wait()
    await_bytes(vx.at[pl.ds(0, DOC_MAX)], m_r.at[0])
    await_bytes(kx.at[pl.ds(0, DOC_MAX)], m_r.at[1])
    docs = lengths.shape[1]
    until = lax.broadcasted_iota(jnp.int32, (docs, docs), 1) <= lax.broadcasted_iota(
        jnp.int32, (docs, docs), 0
    )
    ends = jnp.sum(jnp.where(until, lengths[...], 0), axis=1, keepdims=True)
    query_pos = c * ROWS + lax.broadcasted_iota(jnp.int32, (1, ROWS), 1)
    begin = jnp.max(jnp.where(ends <= query_pos, ends, 0), axis=0, keepdims=True)
    key_pos = c * ROWS - DOC_MAX + lax.broadcasted_iota(jnp.int32, (ROWS + DOC_MAX, ROWS), 0)
    allowed = (key_pos <= query_pos) & (key_pos >= begin)

    def short_step(j, _):
        cols = columns(j)
        q, do = sq[:, cols], sdo[:, cols]
        out, dq, _, _, weights, grads = attend(q, do, [(kx[:, cols], vx[:, cols], allowed)])
        so[:, cols] = out
        sd[0, :, cols] = dq
        dk = dot(grads[0], q) * FACTOR
        dv = dot(weights[0], do)
        sd[1, :, cols] = dk[DOC_MAX:]
        sd[2, :, cols] = dv[DOC_MAX:]
        rim_out[0, :, cols] = dk[:DOC_MAX].astype(BF16)
        rim_out[1, :, cols] = dv[:DOC_MAX].astype(BF16)
        return 0

    lax.fori_loop(0, HEADS, short_step, 0)
    remote(rim_out, rim_in, m_s.at[2], m_r.at[2], before).start()
    pltpu.make_async_copy(so, sout, o_s.at[0]).start()

    def await_mate(s):
        for d in range(4):
            rows = block_rows(lax.rem(x + 4 - d, 4))
            await_bytes(z.at[s, 0, rows], z_r.at[0, s, d])
            await_bytes(z.at[s, 1, rows], z_r.at[1, s, d])

    def put_key_grads(s):
        g[s, 2] = (acc[s, 0] * FACTOR).astype(BF16)
        g[s, 3] = acc[s, 1].astype(BF16)
        send_back(s, 1)

    def later_step(s, _):
        await_mate(s)
        for i in range(2):
            within(s, i, [(z[s, 1], z[s, 0], None)], True)
        remote(stats.at[s], stats_in.at[s], l_s.at[s], l_r.at[s], mate).start()
        send_back(s, 0)
        put_key_grads(s)
        return 0

    def earlier_step(s, _):
        await_mate(s)
        await_bytes(stats_in.at[s], l_r.at[s])
        k, v = t[s, 1], t[s, 2]
        for i in range(2):
            rows = pl.ds(i * 256, 256)
            q, do = z[s, 1, rows], z[s, 0, rows]
            prob = jnp.exp(dot_t(k, q) * FACTOR - stats_in[s, 0:1, rows])
            grad = (prob * (dot_t(v, do) - stats_in[s, 1:2, rows])).astype(BF16)
            acc[s, 0] = acc[s, 0] + dot(grad, q)
            acc[s, 1] = acc[s, 1] + dot(prob.astype(BF16), do)
        put_key_grads(s)
        return 0

    @pl.when(par == 0)
    def _():
        lax.fori_loop(0, count, earlier_step, 0)

    @pl.when(par == 1)
    def _():
        lax.fori_loop(0, count, later_step, 0)

    await_bytes(rim_in, m_r.at[2])

    def fold_step(j, sums_so_far):
        cols = columns(j)
        low = pl.ds(ROWS - DOC_MAX, DOC_MAX)
        sd[1, low, cols] = sd[1, low, cols] + rim_in[0, :, cols].astype(F32)
        sd[2, low, cols] = sd[2, low, cols] + rim_in[1, :, cols].astype(F32)
        fin[5, :, cols] = sd[2, :, cols].astype(BF16)
        a, b = sums_so_far
        a = a + sd[0, :, cols] * gains[0:1, cols] * raw[2, :, cols].astype(F32)
        b = b + sd[1, :, cols] * gains[1:2, cols] * raw[3, :, cols].astype(F32)
        return a, b

    short_sums = lax.fori_loop(0, HEADS, fold_step, (zero, zero))

    def await_back(pair, s, d):
        await_bytes(r.at[pl.ds(2 * pair, 2), :, columns(0)], b_r.at[pair, s, d])

    for pair in range(2):
        for s in range(3):
            for d in range(4):
                if s < 2:
                    await_back(pair, s, d)
                else:
                    pl.when(has_third(x_at(4 - d), core))(
                        lambda pair=pair, s=s, d=d: await_back(pair, s, d)
                    )
    pltpu.make_async_copy(r.at[0], lout, o_s.at[1]).start()
    pltpu.make_async_copy(r.at[3], ldqkv.at[2], o_s.at[2]).start()
    pltpu.make_async_copy(fin.at[5], sdqkv.at[2], o_s.at[3]).start()

    def inner_step(j, sums_so_far):
        cols = columns(j)
        a, b = sums_so_far
        a = a + r[1, :, cols].astype(F32) * gains[0:1, cols] * raw[0, :, cols].astype(F32)
        b = b + r[2, :, cols].astype(F32) * gains[1:2, cols] * raw[1, :, cols].astype(F32)
        return a, b

    long_sums = lax.fori_loop(0, HEADS, inner_step, (zero, zero))
    sums[1] = to_rows([jnp.sum(a, axis=1, keepdims=True) for a in (*long_sums, *short_sums)])
    for d in (1, 2, 3):
        remote(sums.at[1], sums_in.at[1, d], h_s.at[1, d], h_r.at[1, d], head_dev(d)).start()
    for d in (1, 2, 3):
        await_bytes(sums_in.at[1, d], h_r.at[1, d])
    inner = to_cols((sums[1] + sums_in[1, 1] + sums_in[1, 2] + sums_in[1, 3]) / WIDTH)
    scale = inv[...]
    pull = scale * scale * scale * inner

    def final_step(j, _):
        cols = columns(j)
        grads = (r[1, :, cols].astype(F32), r[2, :, cols].astype(F32), sd[0, :, cols], sd[1, :, cols])
        for i in range(4):
            fin[i, :, cols] = (
                scale[:, i : i + 1] * gains[i % 2 : i % 2 + 1, cols] * grads[i]
                - raw[i, :, cols].astype(F32) * pull[:, i : i + 1]
            ).astype(BF16)
        return 0

    lax.fori_loop(0, HEADS, final_step, 0)
    pltpu.make_async_copy(fin.at[pl.ds(0, 2)], ldqkv.at[pl.ds(0, 2)], o_s.at[4]).start()
    pltpu.make_async_copy(fin.at[pl.ds(2, 2)], sdqkv.at[pl.ds(0, 2)], o_s.at[5]).start()

    def left_values(s, d):
        await_bytes(t.at[s, 2, mine], v_s.at[0, s, d])
        await_bytes(t.at[s, 3, mine], v_s.at[1, s, d])
        await_bytes(t.at[s, pl.ds(0, 2), mine], q_s.at[s, d])

    for s in range(3):
        to_peers(s, left_values)

    def left_step(s, _):
        for d in range(4):
            await_bytes(t.at[s, 0, mine], z_s.at[0, s, d])
            await_bytes(t.at[s, 0, mine], z_s.at[1, s, d])
        for d in (1, 2, 3):
            await_bytes(g.at[s, pl.ds(0, 2), mine], b_s.at[0, s, d])
            await_bytes(g.at[s, pl.ds(0, 2), mine], b_s.at[1, s, d])
        pl.when(par == 1)(lambda: await_bytes(stats.at[s], l_s.at[s]))
        return 0

    lax.fori_loop(0, count, left_step, 0)
    for phase in range(2):
        for d in (1, 2, 3):
            await_bytes(sums.at[phase], h_s.at[phase, d])
    await_bytes(vx.at[pl.ds(0, DOC_MAX)], m_s.at[0])
    await_bytes(kx.at[pl.ds(0, DOC_MAX)], m_s.at[1])
    await_bytes(rim_out, m_s.at[2])
    await_bytes(so, o_s.at[0])
    await_bytes(r.at[0], o_s.at[1])
    await_bytes(r.at[3], o_s.at[2])
    await_bytes(fin.at[5], o_s.at[3])
    await_bytes(fin.at[pl.ds(0, 2)], o_s.at[4])
    await_bytes(fin.at[pl.ds(2, 2)], o_s.at[5])


def on_device(long_qkv, long_grad, short_qkv, short_grad, short_lengths, norm_gains):
    anywhere = pl.BlockSpec(memory_space=pl.ANY)
    vmem = pl.BlockSpec(memory_space=pltpu.VMEM)
    wide = (ROWS, LOCAL)
    dma = pltpu.SemaphoreType.DMA
    return pl.pallas_call(
        kernel,
        out_shape=(
            jax.ShapeDtypeStruct(wide, BF16),
            jax.ShapeDtypeStruct((3, *wide), BF16),
            jax.ShapeDtypeStruct(wide, BF16),
            jax.ShapeDtypeStruct((3, *wide), BF16),
        ),
        in_specs=[anywhere] * 4 + [vmem] * 2,
        out_specs=(anywhere,) * 4,
        scratch_shapes=[
            pltpu.VMEM((4, *wide), BF16),
            pltpu.VMEM((2, *wide), BF16),
            pltpu.VMEM(wide, BF16),
            pltpu.VMEM((ROWS + DOC_MAX, LOCAL), BF16),
            pltpu.VMEM((ROWS + DOC_MAX, LOCAL), BF16),
            pltpu.VMEM(wide, BF16),
            pltpu.VMEM((ROWS, HEAD_DIM), F32),
            pltpu.VMEM((2, 8, HEAD_DIM), F32),
            pltpu.VMEM((2, 4, 8, HEAD_DIM), F32),
            pltpu.VMEM((3, 4, HALF, HEAD_DIM), BF16),
            pltpu.VMEM((3, 2, HALF, HEAD_DIM), BF16),
            pltpu.VMEM((3, 8, HALF), F32),
            pltpu.VMEM((3, 8, HALF), F32),
            pltpu.VMEM((3, 4, HALF, HEAD_DIM), BF16),
            pltpu.VMEM((3, 2, HALF, HEAD_DIM), F32),
            pltpu.VMEM((4, *wide), BF16),
            pltpu.VMEM(wide, BF16),
            pltpu.VMEM((3, *wide), F32),
            pltpu.VMEM((2, DOC_MAX, LOCAL), BF16),
            pltpu.VMEM((2, DOC_MAX, LOCAL), BF16),
            pltpu.VMEM((6, *wide), BF16),
            dma((6,)),
            dma((2, 3, 4)),
            dma((2, 3, 4)),
            dma((3, 4)),
            dma((3, 4)),
            dma((2, 3, 4)),
            dma((2, 3, 4)),
            dma((3,)),
            dma((3,)),
            dma((2, 3, 4)),
            dma((2, 3, 4)),
            dma((2, 4)),
            dma((2, 4)),
            dma((3,)),
            dma((3,)),
            dma((6,)),
        ],
        compiler_params=pltpu.CompilerParams(
            collective_id=0, has_side_effects=True, vmem_limit_bytes=50 * 2**20
        ),
    )(long_qkv, long_grad, short_qkv, short_grad, short_lengths.reshape(1, -1), norm_gains)


def solution(mesh):
    return jax.shard_map(
        on_device,
        mesh=mesh,
        in_specs=(
            P(None, "ctx", "head"),
            P("ctx", "head"),
            P(None, "ctx", "head"),
            P("ctx", "head"),
            P(),
            P(None, "head"),
        ),
        out_specs=(
            P("ctx", "head"),
            P(None, "ctx", "head"),
            P("ctx", "head"),
            P(None, "ctx", "head"),
        ),
        check_vma=False,
    )
```

```python
import jax
import jax.numpy as jnp
from jax import lax
from jax.experimental import pallas as pl
from jax.experimental.pallas import tpu as pltpu
from jax.sharding import PartitionSpec as P

MESH = pl.DeviceIdType.MESH
BF16 = jnp.bfloat16
F32 = jnp.float32
HEAD_DIM = 128
WIDTH = 5120
DOC_MAX = 64
STRIP = 16
PIECE = 640
WAVE = 5
ROWS = 128
LOCAL = 1280
HEADS = 10
HALF = 512
EPSILON = 1e-06
NEGATIVE = -1e30
FACTOR = HEAD_DIM ** (-0.5)


def first_head(x, core):
    return lax.div(5 * x + 1 - core, 2)


def has_third(x, core):
    return lax.rem(x + core, 2) == 0


def columns(head):
    return pl.ds(pl.multiple_of(head * HEAD_DIM, HEAD_DIM), HEAD_DIM)


def block_rows(x):
    return pl.ds(pl.multiple_of(x * ROWS, ROWS), ROWS)


def await_bytes(ref, sem):
    pltpu.make_async_copy(ref, ref, sem).wait()


def dot(a, b):
    return jnp.dot(a, b, preferred_element_type=F32)


def dot_t(a, b):
    return lax.dot_general(a, b, (((1,), (1,)), ((), ())), preferred_element_type=F32)


def sweep(step, carry):
    def group(i, c):
        for j in range(WAVE):
            c = step(i * WAVE + j, c)
        return c

    return lax.fori_loop(0, HEADS // WAVE, group, carry)


def attend(items):
    scores = []
    for q, _, pieces in items:
        row = []
        for k, _, mask in pieces:
            one = dot_t(k, q) * FACTOR
            row.append(one if mask is None else jnp.where(mask, one, NEGATIVE))
        scores.append(row)
    slopes = [[dot_t(v, do) for _, v, _ in pieces] for _, do, pieces in items]
    highs, totals, probs = [], [], []
    for row in scores:
        high = jnp.max(row[0], axis=0, keepdims=True)
        for one in row[1:]:
            high = jnp.maximum(high, jnp.max(one, axis=0, keepdims=True))
        highs.append(high)
    powers = [[jnp.exp(one - high) for one in row] for row, high in zip(scores, highs)]
    for row in powers:
        total = jnp.sum(row[0], axis=0, keepdims=True)
        for one in row[1:]:
            total = total + jnp.sum(one, axis=0, keepdims=True)
        totals.append(total)
    log_totals = [high + jnp.log(total) for high, total in zip(highs, totals)]
    shares = [1.0 / total for total in totals]
    probs = [[one * share for one in row] for row, share in zip(powers, shares)]
    weights = [[one.astype(BF16) for one in row] for row in probs]
    outs_t = []
    for (_, _, pieces), row in zip(items, weights):
        out_t = dot(pieces[0][1].T, row[0])
        for (_, v, _), one in zip(pieces[1:], row[1:]):
            out_t = out_t + dot(v.T, one)
        outs_t.append(out_t.astype(BF16))
    outs = [out_t.astype(F32).T.astype(BF16) for out_t in outs_t]
    row_dots = [
        jnp.sum(do.astype(F32).T * out_t.astype(F32), axis=0, keepdims=True)
        for (_, do, _), out_t in zip(items, outs_t)
    ]
    grads = [
        [(one * (slope - row_dot)).astype(BF16) for one, slope in zip(row, slope_row)]
        for row, slope_row, row_dot in zip(probs, slopes, row_dots)
    ]
    dqs = []
    for (_, _, pieces), row in zip(items, grads):
        dq_t = dot(pieces[0][0].T, row[0])
        for (k, _, _), one in zip(pieces[1:], row[1:]):
            dq_t = dq_t + dot(k.T, one)
        dqs.append((dq_t * FACTOR).T)
    return outs, dqs, log_totals, row_dots, weights, grads


def to_rows(cols):
    lane = lax.broadcasted_iota(jnp.int32, (ROWS, HEAD_DIM), 1)
    packed = jnp.zeros((ROWS, HEAD_DIM), F32)
    for i, col in enumerate(cols):
        packed = jnp.where(lane == i, col, packed)
    return packed.T[:8]


def to_cols(rows):
    return jnp.concatenate([rows] * (ROWS // 8), axis=0).T


def kernel(
    lqkv, lgrad, sqkv, sgrad, lengths, gains,
    lout, ldqkv, sout, sdqkv,
    raw, nlong, w, hops, lens, gain, inv, sums, sums_in,
    t, z, stats, stats_in, g, acc, r, so, sd, edge, edge_in, fin,
    load, v_s, v_r, q_s, q_r, z_s, z_r, l_s, l_r, b_s, b_r, h_s, h_r, m_s, m_r, p_s, p_r, f_s, f_r, e_sem, o_s,
):
    c = lax.axis_index("ctx")
    h = lax.axis_index("head")
    x = lax.rem(c, 4)
    row_base = c - x
    par = lax.rem(lax.div(c, 4), 2)
    core = lax.rem(h, 2)
    third = has_third(x, core)
    count = jnp.where(third, 3, 2)
    first = first_head(x, core)
    mate = (c + 4 - 8 * par, h)
    after = (lax.rem(c + 1, 64), h)
    before = (lax.rem(c + 63, 64), h)

    def x_at(d):
        return lax.rem(x + d, 4)

    def x_dev(d):
        return (row_base + x_at(d), h)

    def head_dev(d):
        return (c, lax.rem(h + d, 4))

    def remote(src, dst, send, recv, dev):
        return pltpu.make_async_remote_copy(
            src_ref=src, dst_ref=dst, send_sem=send, recv_sem=recv,
            device_id=dev, device_id_type=MESH,
        )

    loads = [
        pltpu.make_async_copy(lqkv.at[0], raw.at[0], load.at[0]),
        pltpu.make_async_copy(lqkv.at[1], raw.at[1], load.at[1]),
        pltpu.make_async_copy(sqkv.at[0], raw.at[2], load.at[2]),
        pltpu.make_async_copy(sqkv.at[1], raw.at[3], load.at[3]),
        pltpu.make_async_copy(gains, gain, load.at[4]),
        pltpu.make_async_copy(sqkv.at[2], w.at[0, 1, pl.ds(DOC_MAX, ROWS)], load.at[5]),
        pltpu.make_async_copy(sgrad, w.at[1, 1, pl.ds(0, ROWS)], load.at[6]),
        pltpu.make_async_copy(lengths, lens, load.at[7]),
    ]
    for copy in loads:
        copy.start()

    peers = [x_dev(1), x_dev(2), x_dev(3), mate, head_dev(1), head_dev(2), head_dev(3), after, before]
    barrier = pltpu.get_barrier_semaphore()
    for dev in peers:
        pl.semaphore_signal(barrier, inc=1, device_id=dev, device_id_type=MESH)

    mine = block_rows(x)

    def own_values(s):
        for kind, src in ((0, lqkv.at[2]), (1, lgrad)):
            pltpu.make_async_copy(
                src.at[:, columns(first + s)], t.at[s, 2 + kind, mine], v_r.at[kind, s, 0]
            ).start()

    def send_values(s, d):
        for kind, src in ((0, lqkv.at[2]), (1, lgrad)):
            remote(
                src.at[:, columns(first_head(x_at(d), core) + s)], t.at[s, 2 + kind, mine],
                v_s.at[kind, s, d], v_r.at[kind, s, d], x_dev(d),
            ).start()

    def send_keys(s, d):
        remote(
            nlong.at[:, :, columns(first_head(x_at(d), core) + s)], t.at[s, pl.ds(0, 2), mine],
            q_s.at[s, d], q_r.at[s, d], x_dev(d),
        ).start()

    def own_keys(s):
        pltpu.make_async_copy(
            nlong.at[:, :, columns(first + s)], t.at[s, pl.ds(0, 2), mine], q_r.at[s, 0]
        ).start()

    def to_peers(s, send):
        for d in (1, 2, 3):
            if s < 2:
                send(s, d)
            else:
                pl.when(has_third(x_at(d), core))(lambda d=d: send(s, d))

    own_values(0)
    own_values(1)
    pl.when(third)(lambda: own_values(2))

    pl.semaphore_wait(barrier, len(peers))

    to_peers(0, send_values)

    base = ROWS * (1 - par)
    ending = x == 3 - 3 * par
    inner_column = jnp.logical_not(ending)
    meeting = x == 3 * par
    sends_on = jnp.logical_not((par == 0) & (x == 3))
    sends_back = jnp.logical_not((par == 1) & (x == 0))
    last = far = pl.ds(ROWS, DOC_MAX)
    near = pl.ds(0, DOC_MAX)

    def strip(column):
        return pl.ds(pl.multiple_of(base + column * STRIP, STRIP), STRIP)

    def send_rims(part):
        @pl.when(ending)
        def _():
            for d in (1, 2, 3):
                remote(
                    w.at[par, part, strip(x_at(d))], hops.at[part, 0],
                    p_s.at[part, d], p_r.at[part, 0], x_dev(d),
                ).start()
            remote(
                w.at[par, part, strip(x)], hops.at[part, 1], p_s.at[part, 0], p_r.at[part, 1], mate
            ).start()

        @pl.when(sends_on)
        def _():
            remote(
                w.at[0, part, last], w.at[0, part, near], m_s.at[part, 0], m_r.at[part, 0], after
            ).start()

        @pl.when(sends_back)
        def _():
            remote(
                w.at[1, part, near], w.at[1, part, far], m_s.at[part, 1], m_r.at[part, 1], before
            ).start()

    def cross_rims(part):
        @pl.when(inner_column)
        def _():
            await_bytes(hops.at[part, 0], p_r.at[part, 0])

            @pl.when(meeting)
            def _():
                there = pl.ds(pl.multiple_of(ROWS * par + x * STRIP, STRIP), STRIP)
                remote(
                    hops.at[part, 0], w.at[par, part, there],
                    p_s.at[part, 0], f_r.at[part, 0], mate,
                ).start()

            @pl.when(jnp.logical_not(meeting))
            def _():
                remote(
                    hops.at[part, 0], hops.at[part, 1], p_s.at[part, 0], p_r.at[part, 1], mate
                ).start()

    def land_rims(part):
        @pl.when(inner_column)
        def _():
            await_bytes(hops.at[part, 1], p_r.at[part, 1])
            end_d = lax.rem(3 - 3 * par + 4 - x, 4)
            end_dev = (row_base + 3 - 3 * par, h)
            remote(
                hops.at[part, 1], w.at[1 - par, part, strip(x)],
                f_s.at[part], f_r.at[part, end_d], end_dev,
            ).start()

    for copy in loads[5:7]:
        copy.wait()
    send_rims(1)
    to_peers(1, send_values)

    def relay_values(s, d):
        rows = block_rows(lax.rem(x + 4 - d, 4))
        await_bytes(t.at[s, 2, rows], v_r.at[0, s, d])
        await_bytes(t.at[s, 3, rows], v_r.at[1, s, d])
        remote(t.at[s, 2 + par, rows], z.at[s, 0, rows], z_s.at[0, s, d], z_r.at[0, s, d], mate).start()

    def relay_keys(s, d):
        rows = block_rows(lax.rem(x + 4 - d, 4))
        await_bytes(t.at[s, pl.ds(0, 2), rows], q_r.at[s, d])
        remote(t.at[s, 1 - par, rows], z.at[s, 1, rows], z_s.at[1, s, d], z_r.at[1, s, d], mate).start()

    relay_values(0, 0)
    relay_values(1, 0)
    pl.when(third)(lambda: relay_values(2, 0))

    for copy in loads[:5]:
        copy.wait()

    def square_step(j, sums_so_far):
        cols = columns(j)
        new = []
        for i in range(4):
            wide = raw[i, :, cols].astype(F32)
            new.append(sums_so_far[i] + wide * wide)
        return tuple(new)

    zero = jnp.zeros((ROWS, HEAD_DIM), F32)
    squares = sweep(square_step, (zero,) * 4)
    sums[0] = to_rows([jnp.sum(a, axis=1, keepdims=True) for a in squares])
    for d in (1, 2, 3):
        remote(sums.at[0], sums_in.at[0, d], h_s.at[0, d], h_r.at[0, d], head_dev(d)).start()
    for d in (1, 2, 3):
        relay_values(0, d)
    cross_rims(1)
    for d in (1, 2, 3):
        await_bytes(sums_in.at[0, d], h_r.at[0, d])
    all_sums = sums[0] + sums_in[0, 1] + sums_in[0, 2] + sums_in[0, 3]
    inv[...] = to_cols(lax.rsqrt(all_sums / WIDTH + EPSILON))

    spread = [jnp.broadcast_to(inv[:, i : i + 1], (ROWS, HEAD_DIM)) for i in range(4)]

    def normalize_step(j, _):
        cols = columns(j)
        nlong[0, :, cols] = (raw[0, :, cols].astype(F32) * spread[0] * gain[0:1, cols]).astype(BF16)
        nlong[1, :, cols] = (raw[1, :, cols].astype(F32) * spread[1] * gain[1:2, cols]).astype(BF16)
        w[1, 0, pl.ds(0, ROWS), cols] = (
            raw[2, :, cols].astype(F32) * spread[2] * gain[0:1, cols]
        ).astype(BF16)
        w[0, 0, pl.ds(DOC_MAX, ROWS), cols] = (
            raw[3, :, cols].astype(F32) * spread[3] * gain[1:2, cols]
        ).astype(BF16)
        return 0

    sweep(normalize_step, 0)

    send_rims(0)
    own_keys(0)
    own_keys(1)
    pl.when(third)(lambda: own_keys(2))
    to_peers(0, send_keys)
    to_peers(1, send_keys)
    to_peers(2, send_values)
    to_peers(2, send_keys)
    for d in (1, 2, 3):
        relay_values(1, d)
    cross_rims(0)

    diag = lax.broadcasted_iota(jnp.int32, (256, 256), 0) <= lax.broadcasted_iota(
        jnp.int32, (256, 256), 1
    )

    def send_back(s, pair):
        for d in (1, 2, 3):
            remote(
                g.at[s, pl.ds(2 * pair, 2), block_rows(x_at(d))],
                r.at[pl.ds(2 * pair, 2), :, columns(first + s)],
                b_s.at[pair, s, d], b_r.at[pair, s, d], x_dev(d),
            ).start()
        pltpu.make_async_copy(
            g.at[s, pl.ds(2 * pair, 2), mine], r.at[pl.ds(2 * pair, 2), :, columns(first + s)],
            b_r.at[pair, s, 0],
        ).start()

    def within(s, early, keep):
        low, high = pl.ds(0, 256), pl.ds(256, 256)
        pair = [(t[s, 0, rows], t[s, 3, rows]) for rows in (low, high)]
        k_low, v_low = t[s, 1, low], t[s, 2, low]
        items = [
            (*pair[0], [*early, (k_low, v_low, diag)]),
            (*pair[1], [*early, (k_low, v_low, None), (t[s, 1, high], t[s, 2, high], diag)]),
        ]
        outs, dqs, log_totals, row_dots, weights, grads = attend(items)
        for i, rows in enumerate((low, high)):
            g[s, 0, rows] = outs[i]
            g[s, 1, rows] = dqs[i].astype(BF16)
            if keep:
                stats[s, 0:1, rows] = log_totals[i]
                stats[s, 1:2, rows] = row_dots[i]
        at = len(early)
        acc[s, 0, low] = dot(grads[0][at], pair[0][0]) + dot(grads[1][at], pair[1][0])
        acc[s, 1, low] = dot(weights[0][at], pair[0][1]) + dot(weights[1][at], pair[1][1])
        acc[s, 0, high] = dot(grads[1][-1], pair[1][0])
        acc[s, 1, high] = dot(weights[1][-1], pair[1][1])

    def first_half(s):
        @pl.when(par == 0)
        def _():
            within(s, [], False)
            send_back(s, 0)

    def relay_all_keys(s):
        for d in range(4):
            relay_keys(s, d)

    relay_all_keys(0)
    land_rims(1)
    first_half(0)
    relay_all_keys(1)
    land_rims(0)
    first_half(1)

    loads[7].wait()
    docs = lens.shape[1]

    def short_documents():
        for part in range(2):

            @pl.when(sends_back)
            def _():
                await_bytes(w.at[0, part, near], m_r.at[part, 0])

            @pl.when(ending & (par == 1))
            def _():
                for d in range(4):
                    await_bytes(w.at[0, part, pl.ds(0, STRIP)], f_r.at[part, d])

        def short_step(i, _):
            spans = [columns(i * WAVE + j) for j in range(WAVE)]
            own = pl.ds(0, ROWS)
            items = [
                (w[1, 0, own, cols], w[1, 1, own, cols], [(w[0, 0, :, cols], w[0, 1, :, cols], allowed)])
                for cols in spans
            ]
            outs, dqs, log_totals, row_dots, weights, grads = attend(items)
            dks = [dot(grad[0][DOC_MAX:], item[0]) * FACTOR for grad, item in zip(grads, items)]
            dvs = [dot(weight[0][DOC_MAX:], item[1]) for weight, item in zip(weights, items)]
            for j, cols in enumerate(spans):
                so[:, cols] = outs[j]
                sd[0, :, cols] = dqs[j]
                sd[1, :, cols] = dks[j]
                sd[2, :, cols] = dvs[j]
                edge[i * WAVE + j, 0:1] = log_totals[j]
                edge[i * WAVE + j, 1:2] = row_dots[j]
            return 0

        lax.fori_loop(0, HEADS // WAVE, short_step, 0)
        remote(edge, edge_in, e_sem.at[0], e_sem.at[1], before).start()
        pltpu.make_async_copy(so, sout, o_s.at[0]).start()

    def document_begins(first_query, queries):
        query_pos = first_query + lax.broadcasted_iota(jnp.int32, (1, queries), 1)
        return query_pos, jnp.max(jnp.where(ends <= query_pos, ends, 0), axis=0, keepdims=True)

    until = lax.broadcasted_iota(jnp.int32, (docs, docs), 1) <= lax.broadcasted_iota(
        jnp.int32, (docs, docs), 0
    )
    ends = jnp.sum(jnp.where(until, lens[...], 0), axis=1, keepdims=True)
    query_pos, begin = document_begins(c * ROWS, ROWS)
    key_pos = c * ROWS - DOC_MAX + lax.broadcasted_iota(jnp.int32, (ROWS + DOC_MAX, ROWS), 0)
    allowed = (key_pos <= query_pos) & (key_pos >= begin)

    def await_mate(s):
        for d in range(4):
            rows = block_rows(lax.rem(x + 4 - d, 4))
            await_bytes(z.at[s, 0, rows], z_r.at[0, s, d])
            await_bytes(z.at[s, 1, rows], z_r.at[1, s, d])

    def put_key_grads(s):
        g[s, 2] = (acc[s, 0] * FACTOR).astype(BF16)
        g[s, 3] = acc[s, 1].astype(BF16)
        send_back(s, 1)

    def later_step(s):
        await_mate(s)
        within(s, [(z[s, 1], z[s, 0], None)], True)
        remote(stats.at[s], stats_in.at[s], l_s.at[s], l_r.at[s], mate).start()
        send_back(s, 0)
        put_key_grads(s)

    def earlier_step(s):
        await_mate(s)
        await_bytes(stats_in.at[s], l_r.at[s])
        k, v = t[s, 1], t[s, 2]
        for i in range(2):
            rows = pl.ds(i * 256, 256)
            q, do = z[s, 1, rows], z[s, 0, rows]
            prob = jnp.exp(dot_t(k, q) * FACTOR - stats_in[s, 0:1, rows])
            grad = (prob * (dot_t(v, do) - stats_in[s, 1:2, rows])).astype(BF16)
            acc[s, 0] = acc[s, 0] + dot(grad, q)
            acc[s, 1] = acc[s, 1] + dot(prob.astype(BF16), do)
        put_key_grads(s)

    def meet(s):
        pl.when(par == 0)(lambda: earlier_step(s))
        pl.when(par == 1)(lambda: later_step(s))

    short_documents()
    pl.when(par == 1)(lambda: later_step(0))

    @pl.when(third)
    def _():
        for d in (1, 2, 3):
            relay_values(2, d)
        relay_all_keys(2)
        first_half(2)

    pl.when(par == 0)(lambda: earlier_step(0))
    meet(1)

    for part in range(2):

        @pl.when(sends_on)
        def _():
            await_bytes(w.at[1, part, far], m_r.at[part, 1])

        @pl.when(ending & (par == 0))
        def _():
            for d in range(4):
                await_bytes(w.at[1, part, pl.ds(0, STRIP)], f_r.at[part, d])

    await_bytes(edge_in, e_sem.at[1])
    next_begin = document_begins((c + 1) * ROWS, ROWS)[1]
    last_pos = c * ROWS + ROWS - DOC_MAX + lax.broadcasted_iota(jnp.int32, (DOC_MAX, DOC_MAX), 0)
    reached = last_pos >= next_begin[:, :DOC_MAX]

    def fold_step(i, sums_so_far):
        low = pl.ds(ROWS - DOC_MAX, DOC_MAX)
        lanes = pl.ds(0, DOC_MAX)
        spans = [columns(i * WAVE + j) for j in range(WAVE)]
        keys = [(w[0, 0, last, cols], w[0, 1, last, cols]) for cols in spans]
        queries = [(w[1, 0, far, cols], w[1, 1, far, cols]) for cols in spans]
        scores = [dot_t(k, q) * FACTOR for (k, _), (q, _) in zip(keys, queries)]
        slopes = [dot_t(v, do) for (_, v), (_, do) in zip(keys, queries)]
        probs = [
            jnp.where(reached, jnp.exp(one - edge_in[i * WAVE + j, 0:1, lanes]), 0.0)
            for j, one in enumerate(scores)
        ]
        grads = [
            (prob * (slope - edge_in[i * WAVE + j, 1:2, lanes])).astype(BF16)
            for j, (prob, slope) in enumerate(zip(probs, slopes))
        ]
        dks = [dot(grad, q) * FACTOR for grad, (q, _) in zip(grads, queries)]
        dvs = [dot(prob.astype(BF16), do) for prob, (_, do) in zip(probs, queries)]
        a, b = sums_so_far
        for j, cols in enumerate(spans):
            sd[1, low, cols] = sd[1, low, cols] + dks[j]
            sd[2, low, cols] = sd[2, low, cols] + dvs[j]
        for cols in spans:
            fin[5, :, cols] = sd[2, :, cols].astype(BF16)
            a = a + sd[0, :, cols] * gain[0:1, cols] * raw[2, :, cols].astype(F32)
            b = b + sd[1, :, cols] * gain[1:2, cols] * raw[3, :, cols].astype(F32)
        return a, b

    short_sums = lax.fori_loop(0, HEADS // WAVE, fold_step, (zero, zero))
    pltpu.make_async_copy(fin.at[5], sdqkv.at[2], o_s.at[3]).start()

    def start_inner(phase, pair):
        sums[phase] = to_rows([jnp.sum(a, axis=1, keepdims=True) for a in pair])
        for d in (1, 2, 3):
            remote(
                sums.at[phase], sums_in.at[phase, d], h_s.at[phase, d], h_r.at[phase, d], head_dev(d)
            ).start()

    def end_inner(phase, at, grads):
        for d in (1, 2, 3):
            await_bytes(sums_in.at[phase, d], h_r.at[phase, d])
        inner = to_cols(
            (sums[phase] + sums_in[phase, 1] + sums_in[phase, 2] + sums_in[phase, 3]) / WIDTH
        )

        scales = [jnp.broadcast_to(inv[:, at + i : at + i + 1], (ROWS, HEAD_DIM)) for i in range(2)]
        pulls = [
            scale * scale * scale * jnp.broadcast_to(inner[:, i : i + 1], (ROWS, HEAD_DIM))
            for i, scale in enumerate(scales)
        ]

        def final_step(j, _):
            cols = columns(j)
            for i in range(2):
                fin[at + i, :, cols] = (
                    scales[i] * gain[i : i + 1, cols] * grads(i, cols)
                    - raw[at + i, :, cols].astype(F32) * pulls[i]
                ).astype(BF16)
            return 0

        sweep(final_step, 0)

    start_inner(1, short_sums)
    pl.when(third)(lambda: meet(2))
    end_inner(1, 2, lambda i, cols: sd[i, :, cols])
    pltpu.make_async_copy(fin.at[pl.ds(2, 2)], sdqkv.at[pl.ds(0, 2)], o_s.at[5]).start()

    def await_back(pair, s, d):
        await_bytes(r.at[pl.ds(2 * pair, 2), :, columns(0)], b_r.at[pair, s, d])

    for pair in range(2):
        for s in range(3):
            for d in range(4):
                if s < 2:
                    await_back(pair, s, d)
                else:
                    pl.when(has_third(x_at(4 - d), core))(
                        lambda pair=pair, s=s, d=d: await_back(pair, s, d)
                    )
    pltpu.make_async_copy(r.at[0], lout, o_s.at[1]).start()
    pltpu.make_async_copy(r.at[3], ldqkv.at[2], o_s.at[2]).start()
    def inner_step(j, sums_so_far):
        cols = columns(j)
        a, b = sums_so_far
        a = a + r[1, :, cols].astype(F32) * gain[0:1, cols] * raw[0, :, cols].astype(F32)
        b = b + r[2, :, cols].astype(F32) * gain[1:2, cols] * raw[1, :, cols].astype(F32)
        return a, b

    long_sums = sweep(inner_step, (zero, zero))
    start_inner(2, long_sums)
    end_inner(2, 0, lambda i, cols: r[1 + i, :, cols].astype(F32))
    pltpu.make_async_copy(fin.at[pl.ds(0, 2)], ldqkv.at[pl.ds(0, 2)], o_s.at[4]).start()

    def left_values(s, d):
        await_bytes(t.at[s, 2, mine], v_s.at[0, s, d])
        await_bytes(t.at[s, 3, mine], v_s.at[1, s, d])
        await_bytes(t.at[s, pl.ds(0, 2), mine], q_s.at[s, d])

    for s in range(3):
        to_peers(s, left_values)

    def left_step(s, _):
        for d in range(4):
            await_bytes(t.at[s, 0, mine], z_s.at[0, s, d])
            await_bytes(t.at[s, 0, mine], z_s.at[1, s, d])
        for d in (1, 2, 3):
            await_bytes(g.at[s, pl.ds(0, 2), mine], b_s.at[0, s, d])
            await_bytes(g.at[s, pl.ds(0, 2), mine], b_s.at[1, s, d])
        pl.when(par == 1)(lambda: await_bytes(stats.at[s], l_s.at[s]))
        return 0

    lax.fori_loop(0, count, left_step, 0)
    for phase in range(3):
        for d in (1, 2, 3):
            await_bytes(sums.at[phase], h_s.at[phase, d])
    for part in range(2):

        @pl.when(sends_on)
        def _():
            await_bytes(w.at[0, part, last], m_s.at[part, 0])

        @pl.when(sends_back)
        def _():
            await_bytes(w.at[1, part, near], m_s.at[part, 1])

        await_bytes(hops.at[part, 0], p_s.at[part, 0])

        @pl.when(ending)
        def _():
            for d in (1, 2, 3):
                await_bytes(hops.at[part, 0], p_s.at[part, d])

        @pl.when(inner_column)
        def _():
            await_bytes(hops.at[part, 1], f_s.at[part])

    await_bytes(edge, e_sem.at[0])
    await_bytes(so, o_s.at[0])
    await_bytes(r.at[0], o_s.at[1])
    await_bytes(r.at[3], o_s.at[2])
    await_bytes(fin.at[5], o_s.at[3])
    await_bytes(fin.at[pl.ds(0, 2)], o_s.at[4])
    await_bytes(fin.at[pl.ds(2, 2)], o_s.at[5])


def hand_over(a, b, c, d, a_out, b_out, c_out, d_out):
    a_out[...] = a[...]
    b_out[...] = b[...]
    c_out[...] = c[...]
    d_out[...] = d[...]


def on_device(long_qkv, long_grad, short_qkv, short_grad, short_lengths, norm_gains):
    anywhere = pl.BlockSpec(memory_space=pl.ANY)
    wide = (ROWS, LOCAL)
    dma = pltpu.SemaphoreType.DMA
    shapes = (
        jax.ShapeDtypeStruct(wide, BF16),
        jax.ShapeDtypeStruct((3, *wide), BF16),
        jax.ShapeDtypeStruct(wide, BF16),
        jax.ShapeDtypeStruct((3, *wide), BF16),
    )
    results = pl.pallas_call(
        kernel,
        out_shape=shapes,
        in_specs=[anywhere] * 6,
        out_specs=(anywhere,) * 4,
        scratch_shapes=[
            pltpu.VMEM((4, *wide), BF16),
            pltpu.VMEM((2, *wide), BF16),
            pltpu.VMEM((2, 2, ROWS + DOC_MAX, LOCAL), BF16),
            pltpu.VMEM((2, 2, STRIP, LOCAL), BF16),
            pltpu.VMEM((1, 256), jnp.int32),
            pltpu.VMEM((2, LOCAL), F32),
            pltpu.VMEM((ROWS, HEAD_DIM), F32),
            pltpu.VMEM((3, 8, HEAD_DIM), F32),
            pltpu.VMEM((3, 4, 8, HEAD_DIM), F32),
            pltpu.VMEM((3, 4, HALF, HEAD_DIM), BF16),
            pltpu.VMEM((3, 2, HALF, HEAD_DIM), BF16),
            pltpu.VMEM((3, 8, HALF), F32),
            pltpu.VMEM((3, 8, HALF), F32),
            pltpu.VMEM((3, 4, HALF, HEAD_DIM), BF16),
            pltpu.VMEM((3, 2, HALF, HEAD_DIM), F32),
            pltpu.VMEM((4, *wide), BF16),
            pltpu.VMEM(wide, BF16),
            pltpu.VMEM((3, *wide), F32),
            pltpu.VMEM((HEADS, 8, ROWS), F32),
            pltpu.VMEM((HEADS, 8, ROWS), F32),
            pltpu.VMEM((6, *wide), BF16),
            dma((8,)),
            dma((2, 3, 4)),
            dma((2, 3, 4)),
            dma((3, 4)),
            dma((3, 4)),
            dma((2, 3, 4)),
            dma((2, 3, 4)),
            dma((3,)),
            dma((3,)),
            dma((2, 3, 4)),
            dma((2, 3, 4)),
            dma((3, 4)),
            dma((3, 4)),
            dma((2, 2)),
            dma((2, 2)),
            dma((2, 4)),
            dma((2, 2)),
            dma((2,)),
            dma((2, 4)),
            dma((2,)),
            dma((6,)),
        ],
        compiler_params=pltpu.CompilerParams(
            collective_id=0, has_side_effects=True, vmem_limit_bytes=60 * 2**20
        ),
    )(long_qkv, long_grad, short_qkv, short_grad, short_lengths.reshape(1, -1), norm_gains)
    flat = pl.BlockSpec((ROWS, PIECE), lambda i: (0, i))
    stacked = pl.BlockSpec((3, ROWS, PIECE), lambda i: (0, 0, i))
    return pl.pallas_call(
        hand_over,
        grid=(LOCAL // PIECE,),
        out_shape=shapes,
        in_specs=[flat, stacked, flat, stacked],
        out_specs=(flat, stacked, flat, stacked),
    )(*results)


def solution(mesh):
    return jax.shard_map(
        on_device,
        mesh=mesh,
        in_specs=(
            P(None, "ctx", "head"),
            P("ctx", "head"),
            P(None, "ctx", "head"),
            P("ctx", "head"),
            P(),
            P(None, "head"),
        ),
        out_specs=(
            P("ctx", "head"),
            P(None, "ctx", "head"),
            P("ctx", "head"),
            P(None, "ctx", "head"),
        ),
        check_vma=False,
    )
```

```python
import jax
import jax.numpy as jnp
from jax import lax
from jax.experimental import pallas as pl
from jax.experimental.pallas import tpu as pltpu
from jax.sharding import PartitionSpec as P

MESH = pl.DeviceIdType.MESH
BF16 = jnp.bfloat16
F32 = jnp.float32
HEAD_DIM = 128
WIDTH = 5120
DOC_MAX = 64
STRIP = 16
PIECE = 640
WAVE = 5
ROWS = 128
LOCAL = 1280
HEADS = 10
HALF = 512
EPSILON = 1e-06
NEGATIVE = -1e30
FACTOR = HEAD_DIM ** (-0.5)


def first_head(x, core):
    return lax.div(5 * x + 1 - core, 2)


def has_third(x, core):
    return lax.rem(x + core, 2) == 0


def columns(head):
    return pl.ds(pl.multiple_of(head * HEAD_DIM, HEAD_DIM), HEAD_DIM)


def block_rows(x):
    return pl.ds(pl.multiple_of(x * ROWS, ROWS), ROWS)


def await_bytes(ref, sem):
    pltpu.make_async_copy(ref, ref, sem).wait()


def dot(a, b):
    return jnp.dot(a, b, preferred_element_type=F32)


def dot_t(a, b):
    return lax.dot_general(a, b, (((1,), (1,)), ((), ())), preferred_element_type=F32)


def sweep(step, carry):
    def group(i, c):
        for j in range(WAVE):
            c = step(i * WAVE + j, c)
        return c

    return lax.fori_loop(0, HEADS // WAVE, group, carry)


def attend(items):
    scores = []
    for q, _, pieces in items:
        row = []
        for k, _, mask in pieces:
            one = dot_t(k, q) * FACTOR
            row.append(one if mask is None else jnp.where(mask, one, NEGATIVE))
        scores.append(row)
    slopes = [[dot_t(v, do) for _, v, _ in pieces] for _, do, pieces in items]
    highs, totals, probs = [], [], []
    for row in scores:
        high = jnp.max(row[0], axis=0, keepdims=True)
        for one in row[1:]:
            high = jnp.maximum(high, jnp.max(one, axis=0, keepdims=True))
        highs.append(high)
    powers = [[jnp.exp(one - high) for one in row] for row, high in zip(scores, highs)]
    for row in powers:
        total = jnp.sum(row[0], axis=0, keepdims=True)
        for one in row[1:]:
            total = total + jnp.sum(one, axis=0, keepdims=True)
        totals.append(total)
    log_totals = [high + jnp.log(total) for high, total in zip(highs, totals)]
    shares = [1.0 / total for total in totals]
    probs = [[one * share for one in row] for row, share in zip(powers, shares)]
    weights = [[one.astype(BF16) for one in row] for row in probs]
    outs_t = []
    for (_, _, pieces), row in zip(items, weights):
        out_t = dot(pieces[0][1].T, row[0])
        for (_, v, _), one in zip(pieces[1:], row[1:]):
            out_t = out_t + dot(v.T, one)
        outs_t.append(out_t.astype(BF16))
    outs = [out_t.astype(F32).T.astype(BF16) for out_t in outs_t]
    row_dots = [
        jnp.sum(do.astype(F32).T * out_t.astype(F32), axis=0, keepdims=True)
        for (_, do, _), out_t in zip(items, outs_t)
    ]
    grads = [
        [(one * (slope - row_dot)).astype(BF16) for one, slope in zip(row, slope_row)]
        for row, slope_row, row_dot in zip(probs, slopes, row_dots)
    ]
    dqs = []
    for (_, _, pieces), row in zip(items, grads):
        dq_t = dot(pieces[0][0].T, row[0])
        for (k, _, _), one in zip(pieces[1:], row[1:]):
            dq_t = dq_t + dot(k.T, one)
        dqs.append((dq_t * FACTOR).T)
    return outs, dqs, log_totals, row_dots, weights, grads


def to_rows(cols):
    lane = lax.broadcasted_iota(jnp.int32, (ROWS, HEAD_DIM), 1)
    packed = jnp.zeros((ROWS, HEAD_DIM), F32)
    for i, col in enumerate(cols):
        packed = jnp.where(lane == i, col, packed)
    return packed.T[:8]


def to_cols(rows):
    return jnp.concatenate([rows] * (ROWS // 8), axis=0).T


def kernel(
    lqkv, lgrad, sqkv, sgrad, lengths, gains,
    lout, ldqkv, sout, sdqkv,
    raw, nlong, w, hops, lens, gain, inv, sums, sums_in,
    t, z, stats, stats_in, g, acc, r, so, sd, edge, edge_in, fin,
    load, v_s, v_r, q_s, q_r, z_s, z_r, l_s, l_r, b_s, b_r, h_s, h_r, m_s, m_r, p_s, p_r, f_s, f_r, e_sem, o_s,
):
    c = lax.axis_index("ctx")
    h = lax.axis_index("head")
    x = lax.rem(c, 4)
    row_base = c - x
    par = lax.rem(lax.div(c, 4), 2)
    core = lax.rem(h, 2)
    third = has_third(x, core)
    count = jnp.where(third, 3, 2)
    first = first_head(x, core)
    mate = (c + 4 - 8 * par, h)
    after = (lax.rem(c + 1, 64), h)
    before = (lax.rem(c + 63, 64), h)

    def x_at(d):
        return lax.rem(x + d, 4)

    def x_dev(d):
        return (row_base + x_at(d), h)

    def head_dev(d):
        return (c, lax.rem(h + d, 4))

    def remote(src, dst, send, recv, dev):
        return pltpu.make_async_remote_copy(
            src_ref=src, dst_ref=dst, send_sem=send, recv_sem=recv,
            device_id=dev, device_id_type=MESH,
        )

    loads = [
        pltpu.make_async_copy(lqkv.at[0], raw.at[0], load.at[0]),
        pltpu.make_async_copy(lqkv.at[1], raw.at[1], load.at[1]),
        pltpu.make_async_copy(sqkv.at[0], raw.at[2], load.at[2]),
        pltpu.make_async_copy(sqkv.at[1], raw.at[3], load.at[3]),
        pltpu.make_async_copy(gains, gain, load.at[4]),
        pltpu.make_async_copy(sqkv.at[2], w.at[0, 1, pl.ds(DOC_MAX, ROWS)], load.at[5]),
        pltpu.make_async_copy(sgrad, w.at[1, 1, pl.ds(0, ROWS)], load.at[6]),
        pltpu.make_async_copy(lengths, lens, load.at[7]),
    ]
    for copy in loads:
        copy.start()

    peers = [x_dev(1), x_dev(2), x_dev(3), mate, head_dev(1), head_dev(2), head_dev(3)]
    is_first, is_last = c == 0, c == 63
    leaves = (x == 3) & jnp.logical_not(is_last)
    enters = (x == 0) & jnp.logical_not(is_first)
    barrier = pltpu.get_barrier_semaphore()
    for dev in peers:
        pl.semaphore_signal(barrier, inc=1, device_id=dev, device_id_type=MESH)

    @pl.when(leaves)
    def _():
        pl.semaphore_signal(barrier, inc=1, device_id=after, device_id_type=MESH)

    @pl.when(enters)
    def _():
        pl.semaphore_signal(barrier, inc=1, device_id=before, device_id_type=MESH)

    mine = block_rows(x)

    def own_values(s):
        for kind, src in ((0, lqkv.at[2]), (1, lgrad)):
            pltpu.make_async_copy(
                src.at[:, columns(first + s)], t.at[s, 2 + kind, mine], v_r.at[kind, s, 0]
            ).start()

    def send_values(s, d):
        for kind, src in ((0, lqkv.at[2]), (1, lgrad)):
            remote(
                src.at[:, columns(first_head(x_at(d), core) + s)], t.at[s, 2 + kind, mine],
                v_s.at[kind, s, d], v_r.at[kind, s, d], x_dev(d),
            ).start()

    def send_keys(s, d):
        remote(
            nlong.at[:, :, columns(first_head(x_at(d), core) + s)], t.at[s, pl.ds(0, 2), mine],
            q_s.at[s, d], q_r.at[s, d], x_dev(d),
        ).start()

    def own_keys(s):
        pltpu.make_async_copy(
            nlong.at[:, :, columns(first + s)], t.at[s, pl.ds(0, 2), mine], q_r.at[s, 0]
        ).start()

    def to_peers(s, send):
        for d in (1, 2, 3):
            if s < 2:
                send(s, d)
            else:
                pl.when(has_third(x_at(d), core))(lambda d=d: send(s, d))

    @pl.when(is_first)
    def _():
        w[0, :, pl.ds(0, DOC_MAX)] = jnp.zeros((2, DOC_MAX, LOCAL), BF16)

    @pl.when(is_last)
    def _():
        w[1, :, pl.ds(ROWS, DOC_MAX)] = jnp.zeros((2, DOC_MAX, LOCAL), BF16)
        edge_in[...] = jnp.zeros_like(edge_in)

    own_values(0)
    own_values(1)
    pl.when(third)(lambda: own_values(2))

    pl.semaphore_wait(barrier, len(peers) + jnp.where(leaves | enters, 1, 0))

    to_peers(0, send_values)

    base = ROWS * (1 - par)
    ending = x == 3 - 3 * par
    inner_column = jnp.logical_not(ending)
    meeting = x == 3 * par
    sends_on = jnp.logical_not(((par == 0) & (x == 3)) | is_last)
    sends_back = jnp.logical_not(((par == 1) & (x == 0)) | is_first)
    last = far = pl.ds(ROWS, DOC_MAX)
    near = pl.ds(0, DOC_MAX)

    def strip(column):
        return pl.ds(pl.multiple_of(base + column * STRIP, STRIP), STRIP)

    def send_rims(part):
        @pl.when(ending)
        def _():
            for d in (1, 2, 3):
                remote(
                    w.at[par, part, strip(x_at(d))], hops.at[part, 0],
                    p_s.at[part, d], p_r.at[part, 0], x_dev(d),
                ).start()
            remote(
                w.at[par, part, strip(x)], hops.at[part, 1], p_s.at[part, 0], p_r.at[part, 1], mate
            ).start()

        @pl.when(sends_on)
        def _():
            remote(
                w.at[0, part, last], w.at[0, part, near], m_s.at[part, 0], m_r.at[part, 0], after
            ).start()

        @pl.when(sends_back)
        def _():
            remote(
                w.at[1, part, near], w.at[1, part, far], m_s.at[part, 1], m_r.at[part, 1], before
            ).start()

    def cross_rims(part):
        @pl.when(inner_column)
        def _():
            await_bytes(hops.at[part, 0], p_r.at[part, 0])

            @pl.when(meeting)
            def _():
                there = pl.ds(pl.multiple_of(ROWS * par + x * STRIP, STRIP), STRIP)
                remote(
                    hops.at[part, 0], w.at[par, part, there],
                    p_s.at[part, 0], f_r.at[part, 0], mate,
                ).start()

            @pl.when(jnp.logical_not(meeting))
            def _():
                remote(
                    hops.at[part, 0], hops.at[part, 1], p_s.at[part, 0], p_r.at[part, 1], mate
                ).start()

    def land_rims(part):
        @pl.when(inner_column)
        def _():
            await_bytes(hops.at[part, 1], p_r.at[part, 1])
            end_d = lax.rem(3 - 3 * par + 4 - x, 4)
            end_dev = (row_base + 3 - 3 * par, h)
            remote(
                hops.at[part, 1], w.at[1 - par, part, strip(x)],
                f_s.at[part], f_r.at[part, end_d], end_dev,
            ).start()

    for copy in loads[5:7]:
        copy.wait()
    send_rims(1)
    to_peers(1, send_values)

    def relay_values(s, d):
        rows = block_rows(lax.rem(x + 4 - d, 4))
        await_bytes(t.at[s, 2, rows], v_r.at[0, s, d])
        await_bytes(t.at[s, 3, rows], v_r.at[1, s, d])
        remote(t.at[s, 2 + par, rows], z.at[s, 0, rows], z_s.at[0, s, d], z_r.at[0, s, d], mate).start()

    def relay_keys(s, d):
        rows = block_rows(lax.rem(x + 4 - d, 4))
        await_bytes(t.at[s, pl.ds(0, 2), rows], q_r.at[s, d])
        remote(t.at[s, 1 - par, rows], z.at[s, 1, rows], z_s.at[1, s, d], z_r.at[1, s, d], mate).start()

    relay_values(0, 0)
    relay_values(1, 0)
    pl.when(third)(lambda: relay_values(2, 0))

    for copy in loads[:5]:
        copy.wait()

    def square_step(j, sums_so_far):
        cols = columns(j)
        new = []
        for i in range(4):
            wide = raw[i, :, cols].astype(F32)
            new.append(sums_so_far[i] + wide * wide)
        return tuple(new)

    zero = jnp.zeros((ROWS, HEAD_DIM), F32)
    squares = sweep(square_step, (zero,) * 4)
    sums[0] = to_rows([jnp.sum(a, axis=1, keepdims=True) for a in squares])
    for d in (1, 2, 3):
        remote(sums.at[0], sums_in.at[0, d], h_s.at[0, d], h_r.at[0, d], head_dev(d)).start()
    for d in (1, 2, 3):
        relay_values(0, d)
    for d in (1, 2, 3):
        await_bytes(sums_in.at[0, d], h_r.at[0, d])
    all_sums = sums[0] + sums_in[0, 1] + sums_in[0, 2] + sums_in[0, 3]
    inv[...] = to_cols(lax.rsqrt(all_sums / WIDTH + EPSILON))

    spread = [jnp.broadcast_to(inv[:, i : i + 1], (ROWS, HEAD_DIM)) for i in range(4)]

    def normalize_step(j, _):
        cols = columns(j)
        nlong[0, :, cols] = (raw[0, :, cols].astype(F32) * spread[0] * gain[0:1, cols]).astype(BF16)
        nlong[1, :, cols] = (raw[1, :, cols].astype(F32) * spread[1] * gain[1:2, cols]).astype(BF16)
        w[1, 0, pl.ds(0, ROWS), cols] = (
            raw[2, :, cols].astype(F32) * spread[2] * gain[0:1, cols]
        ).astype(BF16)
        w[0, 0, pl.ds(DOC_MAX, ROWS), cols] = (
            raw[3, :, cols].astype(F32) * spread[3] * gain[1:2, cols]
        ).astype(BF16)
        return 0

    sweep(normalize_step, 0)

    send_rims(0)
    own_keys(0)
    own_keys(1)
    pl.when(third)(lambda: own_keys(2))
    to_peers(0, send_keys)
    to_peers(1, send_keys)
    to_peers(2, send_values)
    to_peers(2, send_keys)
    cross_rims(1)
    for d in (1, 2, 3):
        relay_values(1, d)
    cross_rims(0)

    diag = lax.broadcasted_iota(jnp.int32, (256, 256), 0) <= lax.broadcasted_iota(
        jnp.int32, (256, 256), 1
    )

    def send_back(s, pair):
        for d in (1, 2, 3):
            remote(
                g.at[s, pl.ds(2 * pair, 2), block_rows(x_at(d))],
                r.at[pl.ds(2 * pair, 2), :, columns(first + s)],
                b_s.at[pair, s, d], b_r.at[pair, s, d], x_dev(d),
            ).start()
        pltpu.make_async_copy(
            g.at[s, pl.ds(2 * pair, 2), mine], r.at[pl.ds(2 * pair, 2), :, columns(first + s)],
            b_r.at[pair, s, 0],
        ).start()

    def within(s, early, keep):
        low, high = pl.ds(0, 256), pl.ds(256, 256)
        pair = [(t[s, 0, rows], t[s, 3, rows]) for rows in (low, high)]
        k_low, v_low = t[s, 1, low], t[s, 2, low]
        items = [
            (*pair[0], [*early, (k_low, v_low, diag)]),
            (*pair[1], [*early, (k_low, v_low, None), (t[s, 1, high], t[s, 2, high], diag)]),
        ]
        outs, dqs, log_totals, row_dots, weights, grads = attend(items)
        for i, rows in enumerate((low, high)):
            g[s, 0, rows] = outs[i]
            g[s, 1, rows] = dqs[i].astype(BF16)
            if keep:
                stats[s, 0:1, rows] = log_totals[i]
                stats[s, 1:2, rows] = row_dots[i]
        at = len(early)
        acc[s, 0, low] = dot(grads[0][at], pair[0][0]) + dot(grads[1][at], pair[1][0])
        acc[s, 1, low] = dot(weights[0][at], pair[0][1]) + dot(weights[1][at], pair[1][1])
        acc[s, 0, high] = dot(grads[1][-1], pair[1][0])
        acc[s, 1, high] = dot(weights[1][-1], pair[1][1])

    def first_half(s):
        @pl.when(par == 0)
        def _():
            within(s, [], False)
            send_back(s, 0)

    def relay_all_keys(s):
        for d in range(4):
            relay_keys(s, d)

    relay_all_keys(0)
    land_rims(1)
    first_half(0)
    relay_all_keys(1)
    land_rims(0)
    first_half(1)

    @pl.when(third)
    def _():
        for d in (1, 2, 3):
            relay_values(2, d)
        relay_all_keys(2)
        first_half(2)

    loads[7].wait()
    docs = lens.shape[1]

    def send_edge():
        remote(edge, edge_in, e_sem.at[0], e_sem.at[1], before).start()

    def short_documents():
        for part in range(2):

            @pl.when(sends_back)
            def _():
                await_bytes(w.at[0, part, near], m_r.at[part, 0])

            @pl.when(ending & (par == 1))
            def _():
                for d in range(4):
                    await_bytes(w.at[0, part, pl.ds(0, STRIP)], f_r.at[part, d])

        def short_step(i, _):
            spans = [columns(i * WAVE + j) for j in range(WAVE)]
            own = pl.ds(0, ROWS)
            items = [
                (w[1, 0, own, cols], w[1, 1, own, cols], [(w[0, 0, :, cols], w[0, 1, :, cols], allowed)])
                for cols in spans
            ]
            outs, dqs, log_totals, row_dots, weights, grads = attend(items)
            dks = [dot(grad[0][DOC_MAX:], item[0]) * FACTOR for grad, item in zip(grads, items)]
            dvs = [dot(weight[0][DOC_MAX:], item[1]) for weight, item in zip(weights, items)]
            for j, cols in enumerate(spans):
                so[:, cols] = outs[j]
                sd[0, :, cols] = dqs[j]
                sd[1, :, cols] = dks[j]
                sd[2, :, cols] = dvs[j]
                edge[i * WAVE + j, 0:1] = log_totals[j]
                edge[i * WAVE + j, 1:2] = row_dots[j]
            return 0

        lax.fori_loop(0, HEADS // WAVE, short_step, 0)
        pl.when(jnp.logical_not(is_first))(lambda: send_edge())
        pltpu.make_async_copy(so, sout, o_s.at[0]).start()

    def document_begins(first_query, queries):
        query_pos = first_query + lax.broadcasted_iota(jnp.int32, (1, queries), 1)
        return query_pos, jnp.max(jnp.where(ends <= query_pos, ends, 0), axis=0, keepdims=True)

    until = lax.broadcasted_iota(jnp.int32, (docs, docs), 1) <= lax.broadcasted_iota(
        jnp.int32, (docs, docs), 0
    )
    ends = jnp.sum(jnp.where(until, lens[...], 0), axis=1, keepdims=True)
    query_pos, begin = document_begins(c * ROWS, ROWS)
    key_pos = c * ROWS - DOC_MAX + lax.broadcasted_iota(jnp.int32, (ROWS + DOC_MAX, ROWS), 0)
    allowed = (key_pos <= query_pos) & (key_pos >= begin)

    def await_mate(s):
        for d in range(4):
            rows = block_rows(lax.rem(x + 4 - d, 4))
            await_bytes(z.at[s, 0, rows], z_r.at[0, s, d])
            await_bytes(z.at[s, 1, rows], z_r.at[1, s, d])

    def put_key_grads(s):
        g[s, 2] = (acc[s, 0] * FACTOR).astype(BF16)
        g[s, 3] = acc[s, 1].astype(BF16)
        send_back(s, 1)

    def later_step(s):
        await_mate(s)
        within(s, [(z[s, 1], z[s, 0], None)], True)
        remote(stats.at[s], stats_in.at[s], l_s.at[s], l_r.at[s], mate).start()
        send_back(s, 0)
        put_key_grads(s)

    def earlier_step(s):
        await_mate(s)
        await_bytes(stats_in.at[s], l_r.at[s])
        k, v = t[s, 1], t[s, 2]
        for i in range(2):
            rows = pl.ds(i * 256, 256)
            q, do = z[s, 1, rows], z[s, 0, rows]
            prob = jnp.exp(dot_t(k, q) * FACTOR - stats_in[s, 0:1, rows])
            grad = (prob * (dot_t(v, do) - stats_in[s, 1:2, rows])).astype(BF16)
            acc[s, 0] = acc[s, 0] + dot(grad, q)
            acc[s, 1] = acc[s, 1] + dot(prob.astype(BF16), do)
        put_key_grads(s)

    def meet(s):
        pl.when(par == 0)(lambda: earlier_step(s))
        pl.when(par == 1)(lambda: later_step(s))

    short_documents()
    pl.when(par == 1)(lambda: later_step(0))

    pl.when(par == 0)(lambda: earlier_step(0))
    meet(1)

    for part in range(2):

        @pl.when(sends_on)
        def _():
            await_bytes(w.at[1, part, far], m_r.at[part, 1])

        @pl.when(ending & (par == 0))
        def _():
            for d in range(4):
                await_bytes(w.at[1, part, pl.ds(0, STRIP)], f_r.at[part, d])

    pl.when(jnp.logical_not(is_last))(lambda: await_bytes(edge_in, e_sem.at[1]))
    next_begin = document_begins((c + 1) * ROWS, ROWS)[1]
    last_pos = c * ROWS + ROWS - DOC_MAX + lax.broadcasted_iota(jnp.int32, (DOC_MAX, DOC_MAX), 0)
    reached = last_pos >= next_begin[:, :DOC_MAX]

    def fold_step(i, sums_so_far):
        low = pl.ds(ROWS - DOC_MAX, DOC_MAX)
        lanes = pl.ds(0, DOC_MAX)
        spans = [columns(i * WAVE + j) for j in range(WAVE)]
        keys = [(w[0, 0, last, cols], w[0, 1, last, cols]) for cols in spans]
        queries = [(w[1, 0, far, cols], w[1, 1, far, cols]) for cols in spans]
        scores = [dot_t(k, q) * FACTOR for (k, _), (q, _) in zip(keys, queries)]
        slopes = [dot_t(v, do) for (_, v), (_, do) in zip(keys, queries)]
        probs = [
            jnp.where(reached, jnp.exp(one - edge_in[i * WAVE + j, 0:1, lanes]), 0.0)
            for j, one in enumerate(scores)
        ]
        grads = [
            (prob * (slope - edge_in[i * WAVE + j, 1:2, lanes])).astype(BF16)
            for j, (prob, slope) in enumerate(zip(probs, slopes))
        ]
        dks = [dot(grad, q) * FACTOR for grad, (q, _) in zip(grads, queries)]
        dvs = [dot(prob.astype(BF16), do) for prob, (_, do) in zip(probs, queries)]
        a, b = sums_so_far
        for j, cols in enumerate(spans):
            sd[1, low, cols] = sd[1, low, cols] + dks[j]
            sd[2, low, cols] = sd[2, low, cols] + dvs[j]
        for cols in spans:
            fin[5, :, cols] = sd[2, :, cols].astype(BF16)
            a = a + sd[0, :, cols] * gain[0:1, cols] * raw[2, :, cols].astype(F32)
            b = b + sd[1, :, cols] * gain[1:2, cols] * raw[3, :, cols].astype(F32)
        return a, b

    short_sums = lax.fori_loop(0, HEADS // WAVE, fold_step, (zero, zero))
    pltpu.make_async_copy(fin.at[5], sdqkv.at[2], o_s.at[3]).start()

    def start_inner(phase, pair):
        sums[phase] = to_rows([jnp.sum(a, axis=1, keepdims=True) for a in pair])
        for d in (1, 2, 3):
            remote(
                sums.at[phase], sums_in.at[phase, d], h_s.at[phase, d], h_r.at[phase, d], head_dev(d)
            ).start()

    def end_inner(phase, at, grads):
        for d in (1, 2, 3):
            await_bytes(sums_in.at[phase, d], h_r.at[phase, d])
        inner = to_cols(
            (sums[phase] + sums_in[phase, 1] + sums_in[phase, 2] + sums_in[phase, 3]) / WIDTH
        )

        scales = [jnp.broadcast_to(inv[:, at + i : at + i + 1], (ROWS, HEAD_DIM)) for i in range(2)]
        pulls = [
            scale * scale * scale * jnp.broadcast_to(inner[:, i : i + 1], (ROWS, HEAD_DIM))
            for i, scale in enumerate(scales)
        ]

        def final_step(j, _):
            cols = columns(j)
            for i in range(2):
                fin[at + i, :, cols] = (
                    scales[i] * gain[i : i + 1, cols] * grads(i, cols)
                    - raw[at + i, :, cols].astype(F32) * pulls[i]
                ).astype(BF16)
            return 0

        sweep(final_step, 0)

    start_inner(1, short_sums)
    pl.when(third)(lambda: meet(2))
    end_inner(1, 2, lambda i, cols: sd[i, :, cols])
    pltpu.make_async_copy(fin.at[pl.ds(2, 2)], sdqkv.at[pl.ds(0, 2)], o_s.at[5]).start()

    def await_back(pair, s, d):
        await_bytes(r.at[pl.ds(2 * pair, 2), :, columns(0)], b_r.at[pair, s, d])

    for pair in range(2):
        for s in range(3):
            for d in range(4):
                if s < 2:
                    await_back(pair, s, d)
                else:
                    pl.when(has_third(x_at(4 - d), core))(
                        lambda pair=pair, s=s, d=d: await_back(pair, s, d)
                    )
    pltpu.make_async_copy(r.at[0], lout, o_s.at[1]).start()
    pltpu.make_async_copy(r.at[3], ldqkv.at[2], o_s.at[2]).start()
    def inner_step(j, sums_so_far):
        cols = columns(j)
        a, b = sums_so_far
        a = a + r[1, :, cols].astype(F32) * gain[0:1, cols] * raw[0, :, cols].astype(F32)
        b = b + r[2, :, cols].astype(F32) * gain[1:2, cols] * raw[1, :, cols].astype(F32)
        return a, b

    long_sums = sweep(inner_step, (zero, zero))
    start_inner(2, long_sums)
    end_inner(2, 0, lambda i, cols: r[1 + i, :, cols].astype(F32))
    pltpu.make_async_copy(fin.at[pl.ds(0, 2)], ldqkv.at[pl.ds(0, 2)], o_s.at[4]).start()

    def left_values(s, d):
        await_bytes(t.at[s, 2, mine], v_s.at[0, s, d])
        await_bytes(t.at[s, 3, mine], v_s.at[1, s, d])
        await_bytes(t.at[s, pl.ds(0, 2), mine], q_s.at[s, d])

    for s in range(3):
        to_peers(s, left_values)

    def left_step(s, _):
        for d in range(4):
            await_bytes(t.at[s, 0, mine], z_s.at[0, s, d])
            await_bytes(t.at[s, 0, mine], z_s.at[1, s, d])
        for d in (1, 2, 3):
            await_bytes(g.at[s, pl.ds(0, 2), mine], b_s.at[0, s, d])
            await_bytes(g.at[s, pl.ds(0, 2), mine], b_s.at[1, s, d])
        pl.when(par == 1)(lambda: await_bytes(stats.at[s], l_s.at[s]))
        return 0

    lax.fori_loop(0, count, left_step, 0)
    for phase in range(3):
        for d in (1, 2, 3):
            await_bytes(sums.at[phase], h_s.at[phase, d])
    for part in range(2):

        @pl.when(sends_on)
        def _():
            await_bytes(w.at[0, part, last], m_s.at[part, 0])

        @pl.when(sends_back)
        def _():
            await_bytes(w.at[1, part, near], m_s.at[part, 1])

        await_bytes(hops.at[part, 0], p_s.at[part, 0])

        @pl.when(ending)
        def _():
            for d in (1, 2, 3):
                await_bytes(hops.at[part, 0], p_s.at[part, d])

        @pl.when(inner_column)
        def _():
            await_bytes(hops.at[part, 1], f_s.at[part])

    pl.when(jnp.logical_not(is_first))(lambda: await_bytes(edge, e_sem.at[0]))
    await_bytes(so, o_s.at[0])
    await_bytes(r.at[0], o_s.at[1])
    await_bytes(r.at[3], o_s.at[2])
    await_bytes(fin.at[5], o_s.at[3])
    await_bytes(fin.at[pl.ds(0, 2)], o_s.at[4])
    await_bytes(fin.at[pl.ds(2, 2)], o_s.at[5])


def hand_over(a, b, c, d, a_out, b_out, c_out, d_out):
    a_out[...] = a[...]
    b_out[...] = b[...]
    c_out[...] = c[...]
    d_out[...] = d[...]


def on_device(long_qkv, long_grad, short_qkv, short_grad, short_lengths, norm_gains):
    anywhere = pl.BlockSpec(memory_space=pl.ANY)
    wide = (ROWS, LOCAL)
    dma = pltpu.SemaphoreType.DMA
    shapes = (
        jax.ShapeDtypeStruct(wide, BF16),
        jax.ShapeDtypeStruct((3, *wide), BF16),
        jax.ShapeDtypeStruct(wide, BF16),
        jax.ShapeDtypeStruct((3, *wide), BF16),
    )
    results = pl.pallas_call(
        kernel,
        out_shape=shapes,
        in_specs=[anywhere] * 6,
        out_specs=(anywhere,) * 4,
        scratch_shapes=[
            pltpu.VMEM((4, *wide), BF16),
            pltpu.VMEM((2, *wide), BF16),
            pltpu.VMEM((2, 2, ROWS + DOC_MAX, LOCAL), BF16),
            pltpu.VMEM((2, 2, STRIP, LOCAL), BF16),
            pltpu.VMEM((1, 256), jnp.int32),
            pltpu.VMEM((2, LOCAL), F32),
            pltpu.VMEM((ROWS, HEAD_DIM), F32),
            pltpu.VMEM((3, 8, HEAD_DIM), F32),
            pltpu.VMEM((3, 4, 8, HEAD_DIM), F32),
            pltpu.VMEM((3, 4, HALF, HEAD_DIM), BF16),
            pltpu.VMEM((3, 2, HALF, HEAD_DIM), BF16),
            pltpu.VMEM((3, 8, HALF), F32),
            pltpu.VMEM((3, 8, HALF), F32),
            pltpu.VMEM((3, 4, HALF, HEAD_DIM), BF16),
            pltpu.VMEM((3, 2, HALF, HEAD_DIM), F32),
            pltpu.VMEM((4, *wide), BF16),
            pltpu.VMEM(wide, BF16),
            pltpu.VMEM((3, *wide), F32),
            pltpu.VMEM((HEADS, 8, ROWS), F32),
            pltpu.VMEM((HEADS, 8, ROWS), F32),
            pltpu.VMEM((6, *wide), BF16),
            dma((8,)),
            dma((2, 3, 4)),
            dma((2, 3, 4)),
            dma((3, 4)),
            dma((3, 4)),
            dma((2, 3, 4)),
            dma((2, 3, 4)),
            dma((3,)),
            dma((3,)),
            dma((2, 3, 4)),
            dma((2, 3, 4)),
            dma((3, 4)),
            dma((3, 4)),
            dma((2, 2)),
            dma((2, 2)),
            dma((2, 4)),
            dma((2, 2)),
            dma((2,)),
            dma((2, 4)),
            dma((2,)),
            dma((6,)),
        ],
        compiler_params=pltpu.CompilerParams(
            collective_id=0, has_side_effects=True, vmem_limit_bytes=60 * 2**20
        ),
    )(long_qkv, long_grad, short_qkv, short_grad, short_lengths.reshape(1, -1), norm_gains)
    flat = pl.BlockSpec((ROWS, PIECE), lambda i: (0, i))
    stacked = pl.BlockSpec((3, ROWS, PIECE), lambda i: (0, 0, i))
    return pl.pallas_call(
        hand_over,
        grid=(LOCAL // PIECE,),
        out_shape=shapes,
        in_specs=[flat, stacked, flat, stacked],
        out_specs=(flat, stacked, flat, stacked),
    )(*results)


def solution(mesh):
    return jax.shard_map(
        on_device,
        mesh=mesh,
        in_specs=(
            P(None, "ctx", "head"),
            P("ctx", "head"),
            P(None, "ctx", "head"),
            P("ctx", "head"),
            P(),
            P(None, "head"),
        ),
        out_specs=(
            P("ctx", "head"),
            P(None, "ctx", "head"),
            P("ctx", "head"),
            P(None, "ctx", "head"),
        ),
        check_vma=False,
    )
```

```python
import jax
import jax.numpy as jnp
from jax import lax
from jax.experimental import pallas as pl
from jax.experimental.pallas import tpu as pltpu
from jax.sharding import PartitionSpec as P

MESH = pl.DeviceIdType.MESH
BF16 = jnp.bfloat16
F32 = jnp.float32
HEAD_DIM = 128
WIDTH = 5120
DOC_MAX = 64
STRIP = 16
PIECE = 640
WAVE = 5
ROWS = 128
LOCAL = 1280
HEADS = 10
HALF = 512
EPSILON = 1e-06
NEGATIVE = -1e30
FACTOR = HEAD_DIM ** (-0.5)


def first_head(x, core):
    return lax.div(5 * x + 1 - core, 2)


def has_third(x, core):
    return lax.rem(x + core, 2) == 0


def columns(head):
    return pl.ds(pl.multiple_of(head * HEAD_DIM, HEAD_DIM), HEAD_DIM)


def block_rows(x):
    return pl.ds(pl.multiple_of(x * ROWS, ROWS), ROWS)


def await_bytes(ref, sem):
    pltpu.make_async_copy(ref, ref, sem).wait()


def dot(a, b):
    return jnp.dot(a, b, preferred_element_type=F32)


def dot_t(a, b):
    return lax.dot_general(a, b, (((1,), (1,)), ((), ())), preferred_element_type=F32)


def sweep(step, carry):
    def group(i, c):
        for j in range(WAVE):
            c = step(i * WAVE + j, c)
        return c

    return lax.fori_loop(0, HEADS // WAVE, group, carry)


def attend(items, on_stats=None):
    scores = []
    for q, _, pieces in items:
        row = []
        for k, _, mask in pieces:
            one = dot_t(k, q) * FACTOR
            row.append(one if mask is None else jnp.where(mask, one, NEGATIVE))
        scores.append(row)
    slopes = [[dot_t(v, do) for _, v, _ in pieces] for _, do, pieces in items]
    highs, totals, probs = [], [], []
    for row in scores:
        high = jnp.max(row[0], axis=0, keepdims=True)
        for one in row[1:]:
            high = jnp.maximum(high, jnp.max(one, axis=0, keepdims=True))
        highs.append(high)
    powers = [[jnp.exp(one - high) for one in row] for row, high in zip(scores, highs)]
    for row in powers:
        total = jnp.sum(row[0], axis=0, keepdims=True)
        for one in row[1:]:
            total = total + jnp.sum(one, axis=0, keepdims=True)
        totals.append(total)
    log_totals = [high + jnp.log(total) for high, total in zip(highs, totals)]
    shares = [1.0 / total for total in totals]
    probs = [[one * share for one in row] for row, share in zip(powers, shares)]
    weights = [[one.astype(BF16) for one in row] for row in probs]
    outs_t = []
    for (_, _, pieces), row in zip(items, weights):
        out_t = dot(pieces[0][1].T, row[0])
        for (_, v, _), one in zip(pieces[1:], row[1:]):
            out_t = out_t + dot(v.T, one)
        outs_t.append(out_t.astype(BF16))
    outs = [out_t.astype(F32).T.astype(BF16) for out_t in outs_t]
    row_dots = [
        jnp.sum(do.astype(F32).T * out_t.astype(F32), axis=0, keepdims=True)
        for (_, do, _), out_t in zip(items, outs_t)
    ]
    if on_stats is not None:
        on_stats(outs, log_totals, row_dots)
    grads = [
        [(one * (slope - row_dot)).astype(BF16) for one, slope in zip(row, slope_row)]
        for row, slope_row, row_dot in zip(probs, slopes, row_dots)
    ]
    dqs = []
    for (_, _, pieces), row in zip(items, grads):
        dq_t = dot(pieces[0][0].T, row[0])
        for (k, _, _), one in zip(pieces[1:], row[1:]):
            dq_t = dq_t + dot(k.T, one)
        dqs.append((dq_t * FACTOR).T)
    return outs, dqs, log_totals, row_dots, weights, grads


def to_rows(cols):
    lane = lax.broadcasted_iota(jnp.int32, (ROWS, HEAD_DIM), 1)
    packed = jnp.zeros((ROWS, HEAD_DIM), F32)
    for i, col in enumerate(cols):
        packed = jnp.where(lane == i, col, packed)
    return packed.T[:8]


def to_cols(rows):
    return jnp.concatenate([rows] * (ROWS // 8), axis=0).T


def kernel(
    lqkv, lgrad, sqkv, sgrad, lengths, gains,
    lout, ldqkv, sout, sdqkv,
    raw, nlong, w, hops, lens, gain, inv, sums, sums_in,
    t, z, stats, stats_in, g, acc, r, so, sd, edge, edge_in, fin,
    load, v_s, v_r, q_s, q_r, z_s, z_r, l_s, l_r, b_s, b_r, h_s, h_r, m_s, m_r, p_s, p_r, f_s, f_r, e_sem, o_s,
):
    c = lax.axis_index("ctx")
    h = lax.axis_index("head")
    x = lax.rem(c, 4)
    row_base = c - x
    par = lax.rem(lax.div(c, 4), 2)
    core = lax.rem(h, 2)
    third = has_third(x, core)
    count = jnp.where(third, 3, 2)
    first = first_head(x, core)
    mate = (c + 4 - 8 * par, h)
    after = (lax.rem(c + 1, 64), h)
    before = (lax.rem(c + 63, 64), h)

    def x_at(d):
        return lax.rem(x + d, 4)

    def x_dev(d):
        return (row_base + x_at(d), h)

    def head_dev(d):
        return (c, lax.rem(h + d, 4))

    def remote(src, dst, send, recv, dev):
        return pltpu.make_async_remote_copy(
            src_ref=src, dst_ref=dst, send_sem=send, recv_sem=recv,
            device_id=dev, device_id_type=MESH,
        )

    loads = [
        pltpu.make_async_copy(lqkv.at[0], raw.at[0], load.at[0]),
        pltpu.make_async_copy(lqkv.at[1], raw.at[1], load.at[1]),
        pltpu.make_async_copy(sqkv.at[0], raw.at[2], load.at[2]),
        pltpu.make_async_copy(sqkv.at[1], raw.at[3], load.at[3]),
        pltpu.make_async_copy(gains, gain, load.at[4]),
        pltpu.make_async_copy(sqkv.at[2], w.at[0, 1, pl.ds(DOC_MAX, ROWS)], load.at[5]),
        pltpu.make_async_copy(sgrad, w.at[1, 1, pl.ds(0, ROWS)], load.at[6]),
        pltpu.make_async_copy(lengths, lens, load.at[7]),
    ]
    for copy in loads:
        copy.start()

    peers = [x_dev(1), x_dev(2), x_dev(3), mate, head_dev(1), head_dev(2), head_dev(3)]
    is_first, is_last = c == 0, c == 63
    leaves = (x == 3) & jnp.logical_not(is_last)
    enters = (x == 0) & jnp.logical_not(is_first)
    barrier = pltpu.get_barrier_semaphore()
    for dev in peers:
        pl.semaphore_signal(barrier, inc=1, device_id=dev, device_id_type=MESH)

    @pl.when(leaves)
    def _():
        pl.semaphore_signal(barrier, inc=1, device_id=after, device_id_type=MESH)

    @pl.when(enters)
    def _():
        pl.semaphore_signal(barrier, inc=1, device_id=before, device_id_type=MESH)

    mine = block_rows(x)

    def own_values(s):
        for kind, src in ((0, lqkv.at[2]), (1, lgrad)):
            pltpu.make_async_copy(
                src.at[:, columns(first + s)], t.at[s, 2 + kind, mine], v_r.at[kind, s, 0]
            ).start()

    def send_values(s, d):
        def send(kind, src):
            remote(
                src.at[:, columns(first_head(x_at(d), core) + s)], t.at[s, 2 + kind, mine],
                v_s.at[kind, s, d], v_r.at[kind, s, d], x_dev(d),
            ).start()

        return send

    def send_raw(s):
        for turn in range(2):
            for kind, src in ((0, lqkv.at[2]), (1, lgrad)):

                @pl.when(par == (kind + turn) % 2)
                def _():
                    to_peers(s, lambda s, d: send_values(s, d)(kind, src))

    def send_keys(s, d):
        remote(
            nlong.at[:, :, columns(first_head(x_at(d), core) + s)], t.at[s, pl.ds(0, 2), mine],
            q_s.at[s, d], q_r.at[s, d], x_dev(d),
        ).start()

    def own_keys(s):
        pltpu.make_async_copy(
            nlong.at[:, :, columns(first + s)], t.at[s, pl.ds(0, 2), mine], q_r.at[s, 0]
        ).start()

    def to_peers(s, send):
        for d in (1, 2, 3):
            if s < 2:
                send(s, d)
            else:
                pl.when(has_third(x_at(d), core))(lambda d=d: send(s, d))

    @pl.when(is_first)
    def _():
        w[0, :, pl.ds(0, DOC_MAX)] = jnp.zeros((2, DOC_MAX, LOCAL), BF16)

    @pl.when(is_last)
    def _():
        w[1, :, pl.ds(ROWS, DOC_MAX)] = jnp.zeros((2, DOC_MAX, LOCAL), BF16)
        edge_in[...] = jnp.zeros_like(edge_in)

    own_values(0)
    own_values(1)
    pl.when(third)(lambda: own_values(2))

    pl.semaphore_wait(barrier, len(peers) + jnp.where(leaves | enters, 1, 0))

    send_raw(0)

    base = ROWS * (1 - par)
    ending = x == 3 - 3 * par
    inner_column = jnp.logical_not(ending)
    meeting = x == 3 * par
    sends_on = jnp.logical_not(((par == 0) & (x == 3)) | is_last)
    sends_back = jnp.logical_not(((par == 1) & (x == 0)) | is_first)
    last = far = pl.ds(ROWS, DOC_MAX)
    near = pl.ds(0, DOC_MAX)

    def strip(column):
        return pl.ds(pl.multiple_of(base + column * STRIP, STRIP), STRIP)

    def send_rims(part):
        @pl.when(ending)
        def _():
            for d in (1, 2, 3):
                remote(
                    w.at[par, part, strip(x_at(d))], hops.at[part, 0],
                    p_s.at[part, d], p_r.at[part, 0], x_dev(d),
                ).start()
            remote(
                w.at[par, part, strip(x)], hops.at[part, 1], p_s.at[part, 0], p_r.at[part, 1], mate
            ).start()

        @pl.when(sends_on)
        def _():
            remote(
                w.at[0, part, last], w.at[0, part, near], m_s.at[part, 0], m_r.at[part, 0], after
            ).start()

        @pl.when(sends_back)
        def _():
            remote(
                w.at[1, part, near], w.at[1, part, far], m_s.at[part, 1], m_r.at[part, 1], before
            ).start()

    def cross_rims(part):
        @pl.when(inner_column)
        def _():
            await_bytes(hops.at[part, 0], p_r.at[part, 0])

            @pl.when(meeting)
            def _():
                there = pl.ds(pl.multiple_of(ROWS * par + x * STRIP, STRIP), STRIP)
                remote(
                    hops.at[part, 0], w.at[par, part, there],
                    p_s.at[part, 0], f_r.at[part, 0], mate,
                ).start()

            @pl.when(jnp.logical_not(meeting))
            def _():
                remote(
                    hops.at[part, 0], hops.at[part, 1], p_s.at[part, 0], p_r.at[part, 1], mate
                ).start()

    def land_rims(part):
        @pl.when(inner_column)
        def _():
            await_bytes(hops.at[part, 1], p_r.at[part, 1])
            end_d = lax.rem(3 - 3 * par + 4 - x, 4)
            end_dev = (row_base + 3 - 3 * par, h)
            remote(
                hops.at[part, 1], w.at[1 - par, part, strip(x)],
                f_s.at[part], f_r.at[part, end_d], end_dev,
            ).start()

    for copy in loads[5:7]:
        copy.wait()
    send_rims(1)
    send_raw(1)

    def relay_values(s, d):
        rows = block_rows(lax.rem(x + 4 - d, 4))
        await_bytes(t.at[s, 2 + par, rows], v_r.at[par, s, d])
        remote(t.at[s, 2 + par, rows], z.at[s, 0, rows], z_s.at[0, s, d], z_r.at[0, s, d], mate).start()

    def relay_keys(s, d):
        rows = block_rows(lax.rem(x + 4 - d, 4))
        await_bytes(t.at[s, pl.ds(0, 2), rows], q_r.at[s, d])
        remote(t.at[s, 1 - par, rows], z.at[s, 1, rows], z_s.at[1, s, d], z_r.at[1, s, d], mate).start()
        await_bytes(t.at[s, 3 - par, rows], v_r.at[1 - par, s, d])

    relay_values(0, 0)
    relay_values(1, 0)
    pl.when(third)(lambda: relay_values(2, 0))

    for copy in loads[:5]:
        copy.wait()

    def square_step(j, sums_so_far):
        cols = columns(j)
        new = []
        for i in range(4):
            wide = raw[i, :, cols].astype(F32)
            new.append(sums_so_far[i] + wide * wide)
        return tuple(new)

    zero = jnp.zeros((ROWS, HEAD_DIM), F32)
    squares = sweep(square_step, (zero,) * 4)
    sums[0] = to_rows([jnp.sum(a, axis=1, keepdims=True) for a in squares])
    for d in (1, 2, 3):
        remote(sums.at[0], sums_in.at[0, d], h_s.at[0, d], h_r.at[0, d], head_dev(d)).start()
    for d in (1, 2, 3):
        relay_values(0, d)
    for d in (1, 2, 3):
        await_bytes(sums_in.at[0, d], h_r.at[0, d])
    all_sums = sums[0] + sums_in[0, 1] + sums_in[0, 2] + sums_in[0, 3]
    inv[...] = to_cols(lax.rsqrt(all_sums / WIDTH + EPSILON))

    spread = [jnp.broadcast_to(inv[:, i : i + 1], (ROWS, HEAD_DIM)) for i in range(4)]

    def normalize_step(j, _):
        cols = columns(j)
        nlong[0, :, cols] = (raw[0, :, cols].astype(F32) * spread[0] * gain[0:1, cols]).astype(BF16)
        nlong[1, :, cols] = (raw[1, :, cols].astype(F32) * spread[1] * gain[1:2, cols]).astype(BF16)
        w[1, 0, pl.ds(0, ROWS), cols] = (
            raw[2, :, cols].astype(F32) * spread[2] * gain[0:1, cols]
        ).astype(BF16)
        w[0, 0, pl.ds(DOC_MAX, ROWS), cols] = (
            raw[3, :, cols].astype(F32) * spread[3] * gain[1:2, cols]
        ).astype(BF16)
        return 0

    sweep(normalize_step, 0)

    send_rims(0)
    own_keys(0)
    own_keys(1)
    pl.when(third)(lambda: own_keys(2))
    to_peers(0, send_keys)
    to_peers(1, send_keys)
    send_raw(2)
    to_peers(2, send_keys)
    cross_rims(1)
    for d in (1, 2, 3):
        relay_values(1, d)
    cross_rims(0)

    diag = lax.broadcasted_iota(jnp.int32, (256, 256), 0) <= lax.broadcasted_iota(
        jnp.int32, (256, 256), 1
    )

    def send_back(s, pair):
        for d in (1, 2, 3):
            remote(
                g.at[s, pl.ds(2 * pair, 2), block_rows(x_at(d))],
                r.at[pl.ds(2 * pair, 2), :, columns(first + s)],
                b_s.at[pair, s, d], b_r.at[pair, s, d], x_dev(d),
            ).start()
        pltpu.make_async_copy(
            g.at[s, pl.ds(2 * pair, 2), mine], r.at[pl.ds(2 * pair, 2), :, columns(first + s)],
            b_r.at[pair, s, 0],
        ).start()

    def within(s, early, keep):
        low, high = pl.ds(0, 256), pl.ds(256, 256)
        pair = [(t[s, 0, rows], t[s, 3, rows]) for rows in (low, high)]
        k_low, v_low = t[s, 1, low], t[s, 2, low]
        items = [
            (*pair[0], [*early, (k_low, v_low, diag)]),
            (*pair[1], [*early, (k_low, v_low, None), (t[s, 1, high], t[s, 2, high], diag)]),
        ]

        def tell(_, log_totals, row_dots):
            for i, rows in enumerate((low, high)):
                stats[s, 0:1, rows] = log_totals[i]
                stats[s, 1:2, rows] = row_dots[i]
            remote(stats.at[s], stats_in.at[s], l_s.at[s], l_r.at[s], mate).start()

        outs, dqs, _, _, weights, grads = attend(items, tell if keep else None)
        for i, rows in enumerate((low, high)):
            g[s, 0, rows] = outs[i]
            g[s, 1, rows] = dqs[i].astype(BF16)
        send_back(s, 0)
        at = len(early)
        acc[s, 0, low] = dot(grads[0][at], pair[0][0]) + dot(grads[1][at], pair[1][0])
        acc[s, 1, low] = dot(weights[0][at], pair[0][1]) + dot(weights[1][at], pair[1][1])
        acc[s, 0, high] = dot(grads[1][-1], pair[1][0])
        acc[s, 1, high] = dot(weights[1][-1], pair[1][1])

    def first_half(s):
        @pl.when(par == 0)
        def _():
            within(s, [], False)

    def relay_all_keys(s):
        for d in range(4):
            relay_keys(s, d)

    relay_all_keys(0)
    land_rims(1)
    first_half(0)
    relay_all_keys(1)
    land_rims(0)
    first_half(1)

    @pl.when(third)
    def _():
        for d in (1, 2, 3):
            relay_values(2, d)
        relay_all_keys(2)
        first_half(2)

    loads[7].wait()
    docs = lens.shape[1]

    def send_edge():
        remote(edge, edge_in, e_sem.at[0], e_sem.at[1], before).start()

    def short_documents():
        for part in range(2):

            @pl.when(sends_back)
            def _():
                await_bytes(w.at[0, part, near], m_r.at[part, 0])

            @pl.when(ending & (par == 1))
            def _():
                for d in range(4):
                    await_bytes(w.at[0, part, pl.ds(0, STRIP)], f_r.at[part, d])

        def short_step(i, _):
            spans = [columns(i * WAVE + j) for j in range(WAVE)]
            own = pl.ds(0, ROWS)
            items = [
                (w[1, 0, own, cols], w[1, 1, own, cols], [(w[0, 0, :, cols], w[0, 1, :, cols], allowed)])
                for cols in spans
            ]
            outs, dqs, log_totals, row_dots, weights, grads = attend(items)
            dks = [dot(grad[0][DOC_MAX:], item[0]) * FACTOR for grad, item in zip(grads, items)]
            dvs = [dot(weight[0][DOC_MAX:], item[1]) for weight, item in zip(weights, items)]
            for j, cols in enumerate(spans):
                so[:, cols] = outs[j]
                sd[0, :, cols] = dqs[j]
                sd[1, :, cols] = dks[j]
                sd[2, :, cols] = dvs[j]
                edge[i * WAVE + j, 0:1] = log_totals[j]
                edge[i * WAVE + j, 1:2] = row_dots[j]
            return 0

        lax.fori_loop(0, HEADS // WAVE, short_step, 0)
        pl.when(jnp.logical_not(is_first))(lambda: send_edge())
        pltpu.make_async_copy(so, sout, o_s.at[0]).start()

    def document_begins(first_query, queries):
        query_pos = first_query + lax.broadcasted_iota(jnp.int32, (1, queries), 1)
        return query_pos, jnp.max(jnp.where(ends <= query_pos, ends, 0), axis=0, keepdims=True)

    until = lax.broadcasted_iota(jnp.int32, (docs, docs), 1) <= lax.broadcasted_iota(
        jnp.int32, (docs, docs), 0
    )
    ends = jnp.sum(jnp.where(until, lens[...], 0), axis=1, keepdims=True)
    query_pos, begin = document_begins(c * ROWS, ROWS)
    key_pos = c * ROWS - DOC_MAX + lax.broadcasted_iota(jnp.int32, (ROWS + DOC_MAX, ROWS), 0)
    allowed = (key_pos <= query_pos) & (key_pos >= begin)

    def await_mate(s):
        for d in range(4):
            rows = block_rows(lax.rem(x + 4 - d, 4))
            await_bytes(z.at[s, 0, rows], z_r.at[0, s, d])
            await_bytes(z.at[s, 1, rows], z_r.at[1, s, d])

    def put_key_grads(s):
        g[s, 2] = (acc[s, 0] * FACTOR).astype(BF16)
        g[s, 3] = acc[s, 1].astype(BF16)
        send_back(s, 1)

    def later_step(s):
        await_mate(s)
        within(s, [(z[s, 1], z[s, 0], None)], True)
        put_key_grads(s)

    def earlier_step(s):
        await_mate(s)
        await_bytes(stats_in.at[s], l_r.at[s])
        k, v = t[s, 1], t[s, 2]
        for i in range(2):
            rows = pl.ds(i * 256, 256)
            q, do = z[s, 1, rows], z[s, 0, rows]
            prob = jnp.exp(dot_t(k, q) * FACTOR - stats_in[s, 0:1, rows])
            grad = (prob * (dot_t(v, do) - stats_in[s, 1:2, rows])).astype(BF16)
            acc[s, 0] = acc[s, 0] + dot(grad, q)
            acc[s, 1] = acc[s, 1] + dot(prob.astype(BF16), do)
        put_key_grads(s)

    def meet(s):
        pl.when(par == 0)(lambda: earlier_step(s))
        pl.when(par == 1)(lambda: later_step(s))

    short_documents()
    pl.when(par == 1)(lambda: later_step(0))

    pl.when(par == 0)(lambda: earlier_step(0))
    meet(1)

    pl.when(third)(lambda: meet(2))

    for part in range(2):

        @pl.when(sends_on)
        def _():
            await_bytes(w.at[1, part, far], m_r.at[part, 1])

        @pl.when(ending & (par == 0))
        def _():
            for d in range(4):
                await_bytes(w.at[1, part, pl.ds(0, STRIP)], f_r.at[part, d])

    pl.when(jnp.logical_not(is_last))(lambda: await_bytes(edge_in, e_sem.at[1]))
    next_begin = document_begins((c + 1) * ROWS, ROWS)[1]
    last_pos = c * ROWS + ROWS - DOC_MAX + lax.broadcasted_iota(jnp.int32, (DOC_MAX, DOC_MAX), 0)
    reached = last_pos >= next_begin[:, :DOC_MAX]

    def fold_step(i, sums_so_far):
        low = pl.ds(ROWS - DOC_MAX, DOC_MAX)
        lanes = pl.ds(0, DOC_MAX)
        spans = [columns(i * WAVE + j) for j in range(WAVE)]
        keys = [(w[0, 0, last, cols], w[0, 1, last, cols]) for cols in spans]
        queries = [(w[1, 0, far, cols], w[1, 1, far, cols]) for cols in spans]
        scores = [dot_t(k, q) * FACTOR for (k, _), (q, _) in zip(keys, queries)]
        slopes = [dot_t(v, do) for (_, v), (_, do) in zip(keys, queries)]
        probs = [
            jnp.where(reached, jnp.exp(one - edge_in[i * WAVE + j, 0:1, lanes]), 0.0)
            for j, one in enumerate(scores)
        ]
        grads = [
            (prob * (slope - edge_in[i * WAVE + j, 1:2, lanes])).astype(BF16)
            for j, (prob, slope) in enumerate(zip(probs, slopes))
        ]
        dks = [dot(grad, q) * FACTOR for grad, (q, _) in zip(grads, queries)]
        dvs = [dot(prob.astype(BF16), do) for prob, (_, do) in zip(probs, queries)]
        a, b = sums_so_far
        for j, cols in enumerate(spans):
            sd[1, low, cols] = sd[1, low, cols] + dks[j]
            sd[2, low, cols] = sd[2, low, cols] + dvs[j]
        for cols in spans:
            fin[5, :, cols] = sd[2, :, cols].astype(BF16)
            a = a + sd[0, :, cols] * gain[0:1, cols] * raw[2, :, cols].astype(F32)
            b = b + sd[1, :, cols] * gain[1:2, cols] * raw[3, :, cols].astype(F32)
        return a, b

    short_sums = lax.fori_loop(0, HEADS // WAVE, fold_step, (zero, zero))
    pltpu.make_async_copy(fin.at[5], sdqkv.at[2], o_s.at[3]).start()

    def start_inner(phase, pair):
        sums[phase] = to_rows([jnp.sum(a, axis=1, keepdims=True) for a in pair])
        for d in (1, 2, 3):
            remote(
                sums.at[phase], sums_in.at[phase, d], h_s.at[phase, d], h_r.at[phase, d], head_dev(d)
            ).start()

    def end_inner(phase, at, grads):
        for d in (1, 2, 3):
            await_bytes(sums_in.at[phase, d], h_r.at[phase, d])
        inner = to_cols(
            (sums[phase] + sums_in[phase, 1] + sums_in[phase, 2] + sums_in[phase, 3]) / WIDTH
        )

        scales = [jnp.broadcast_to(inv[:, at + i : at + i + 1], (ROWS, HEAD_DIM)) for i in range(2)]
        pulls = [
            scale * scale * scale * jnp.broadcast_to(inner[:, i : i + 1], (ROWS, HEAD_DIM))
            for i, scale in enumerate(scales)
        ]

        def final_step(j, _):
            cols = columns(j)
            for i in range(2):
                fin[at + i, :, cols] = (
                    scales[i] * gain[i : i + 1, cols] * grads(i, cols)
                    - raw[at + i, :, cols].astype(F32) * pulls[i]
                ).astype(BF16)
            return 0

        sweep(final_step, 0)

    start_inner(1, short_sums)

    def await_back(pair, s, d):
        await_bytes(r.at[pl.ds(2 * pair, 2), :, columns(0)], b_r.at[pair, s, d])

    for pair in range(2):
        for s in range(3):
            for d in range(4):
                if s < 2:
                    await_back(pair, s, d)
                else:
                    pl.when(has_third(x_at(4 - d), core))(
                        lambda pair=pair, s=s, d=d: await_back(pair, s, d)
                    )
    pltpu.make_async_copy(r.at[0], lout, o_s.at[1]).start()
    pltpu.make_async_copy(r.at[3], ldqkv.at[2], o_s.at[2]).start()
    def inner_step(j, sums_so_far):
        cols = columns(j)
        a, b = sums_so_far
        a = a + r[1, :, cols].astype(F32) * gain[0:1, cols] * raw[0, :, cols].astype(F32)
        b = b + r[2, :, cols].astype(F32) * gain[1:2, cols] * raw[1, :, cols].astype(F32)
        return a, b

    long_sums = sweep(inner_step, (zero, zero))
    start_inner(2, long_sums)
    end_inner(1, 2, lambda i, cols: sd[i, :, cols])
    pltpu.make_async_copy(fin.at[pl.ds(2, 2)], sdqkv.at[pl.ds(0, 2)], o_s.at[5]).start()

    def left_values(s, d):
        await_bytes(t.at[s, 2, mine], v_s.at[0, s, d])
        await_bytes(t.at[s, 3, mine], v_s.at[1, s, d])
        await_bytes(t.at[s, pl.ds(0, 2), mine], q_s.at[s, d])

    for s in range(3):
        to_peers(s, left_values)

    def left_step(s, _):
        for d in range(4):
            await_bytes(t.at[s, 0, mine], z_s.at[0, s, d])
            await_bytes(t.at[s, 0, mine], z_s.at[1, s, d])
        for d in (1, 2, 3):
            await_bytes(g.at[s, pl.ds(0, 2), mine], b_s.at[0, s, d])
            await_bytes(g.at[s, pl.ds(0, 2), mine], b_s.at[1, s, d])
        pl.when(par == 1)(lambda: await_bytes(stats.at[s], l_s.at[s]))
        return 0

    lax.fori_loop(0, count, left_step, 0)
    for part in range(2):

        @pl.when(sends_on)
        def _():
            await_bytes(w.at[0, part, last], m_s.at[part, 0])

        @pl.when(sends_back)
        def _():
            await_bytes(w.at[1, part, near], m_s.at[part, 1])

        await_bytes(hops.at[part, 0], p_s.at[part, 0])

        @pl.when(ending)
        def _():
            for d in (1, 2, 3):
                await_bytes(hops.at[part, 0], p_s.at[part, d])

        @pl.when(inner_column)
        def _():
            await_bytes(hops.at[part, 1], f_s.at[part])

    pl.when(jnp.logical_not(is_first))(lambda: await_bytes(edge, e_sem.at[0]))
    await_bytes(so, o_s.at[0])
    await_bytes(r.at[0], o_s.at[1])
    await_bytes(r.at[3], o_s.at[2])
    await_bytes(fin.at[5], o_s.at[3])

    end_inner(2, 0, lambda i, cols: r[1 + i, :, cols].astype(F32))
    pltpu.make_async_copy(fin.at[pl.ds(0, 2)], ldqkv.at[pl.ds(0, 2)], o_s.at[4]).start()

    for phase in range(3):
        for d in (1, 2, 3):
            await_bytes(sums.at[phase], h_s.at[phase, d])
    await_bytes(fin.at[pl.ds(0, 2)], o_s.at[4])
    await_bytes(fin.at[pl.ds(2, 2)], o_s.at[5])


def hand_over(a, b, c, d, a_out, b_out, c_out, d_out):
    a_out[...] = a[...]
    b_out[...] = b[...]
    c_out[...] = c[...]
    d_out[...] = d[...]


def on_device(long_qkv, long_grad, short_qkv, short_grad, short_lengths, norm_gains):
    anywhere = pl.BlockSpec(memory_space=pl.ANY)
    wide = (ROWS, LOCAL)
    dma = pltpu.SemaphoreType.DMA
    shapes = (
        jax.ShapeDtypeStruct(wide, BF16),
        jax.ShapeDtypeStruct((3, *wide), BF16),
        jax.ShapeDtypeStruct(wide, BF16),
        jax.ShapeDtypeStruct((3, *wide), BF16),
    )
    results = pl.pallas_call(
        kernel,
        out_shape=shapes,
        in_specs=[anywhere] * 6,
        out_specs=(anywhere,) * 4,
        scratch_shapes=[
            pltpu.VMEM((4, *wide), BF16),
            pltpu.VMEM((2, *wide), BF16),
            pltpu.VMEM((2, 2, ROWS + DOC_MAX, LOCAL), BF16),
            pltpu.VMEM((2, 2, STRIP, LOCAL), BF16),
            pltpu.VMEM((1, 256), jnp.int32),
            pltpu.VMEM((2, LOCAL), F32),
            pltpu.VMEM((ROWS, HEAD_DIM), F32),
            pltpu.VMEM((3, 8, HEAD_DIM), F32),
            pltpu.VMEM((3, 4, 8, HEAD_DIM), F32),
            pltpu.VMEM((3, 4, HALF, HEAD_DIM), BF16),
            pltpu.VMEM((3, 2, HALF, HEAD_DIM), BF16),
            pltpu.VMEM((3, 8, HALF), F32),
            pltpu.VMEM((3, 8, HALF), F32),
            pltpu.VMEM((3, 4, HALF, HEAD_DIM), BF16),
            pltpu.VMEM((3, 2, HALF, HEAD_DIM), F32),
            pltpu.VMEM((4, *wide), BF16),
            pltpu.VMEM(wide, BF16),
            pltpu.VMEM((3, *wide), F32),
            pltpu.VMEM((HEADS, 8, ROWS), F32),
            pltpu.VMEM((HEADS, 8, ROWS), F32),
            pltpu.VMEM((6, *wide), BF16),
            dma((8,)),
            dma((2, 3, 4)),
            dma((2, 3, 4)),
            dma((3, 4)),
            dma((3, 4)),
            dma((2, 3, 4)),
            dma((2, 3, 4)),
            dma((3,)),
            dma((3,)),
            dma((2, 3, 4)),
            dma((2, 3, 4)),
            dma((3, 4)),
            dma((3, 4)),
            dma((2, 2)),
            dma((2, 2)),
            dma((2, 4)),
            dma((2, 2)),
            dma((2,)),
            dma((2, 4)),
            dma((2,)),
            dma((6,)),
        ],
        compiler_params=pltpu.CompilerParams(
            collective_id=0, has_side_effects=True, vmem_limit_bytes=60 * 2**20
        ),
    )(long_qkv, long_grad, short_qkv, short_grad, short_lengths.reshape(1, -1), norm_gains)
    flat = pl.BlockSpec((ROWS, PIECE), lambda i: (0, i))
    stacked = pl.BlockSpec((3, ROWS, PIECE), lambda i: (0, 0, i))
    return pl.pallas_call(
        hand_over,
        grid=(LOCAL // PIECE,),
        out_shape=shapes,
        in_specs=[flat, stacked, flat, stacked],
        out_specs=(flat, stacked, flat, stacked),
    )(*results)


def solution(mesh):
    return jax.shard_map(
        on_device,
        mesh=mesh,
        in_specs=(
            P(None, "ctx", "head"),
            P("ctx", "head"),
            P(None, "ctx", "head"),
            P("ctx", "head"),
            P(),
            P(None, "head"),
        ),
        out_specs=(
            P("ctx", "head"),
            P(None, "ctx", "head"),
            P("ctx", "head"),
            P(None, "ctx", "head"),
        ),
        check_vma=False,
    )
```
